1024 devices in a mesh: curve: 256 (over y, z, core), group: 4 (over x).
Axes of the slice: x: 4, y: 4, z: 32, core: 2. Of those that a mesh axis runs over, the one named last changes fastest.
Arguments:
- tangent: float32 [5, 64, 131072], P(None, None, ('curve', 'group')), may hold values from -6 to 6
- flux_jacobian: float32 [3, 5, 5, 131072], P(None, None, None, ('curve', 'group')), may hold values from -1.75 to 1.75
- viscosity: float32 [131072], P(('curve', 'group')), may hold values from 0.02 to 0.2
- neighbours: int32 [6, 131072], P(None, ('curve', 'group')), may hold values from -2 to 131071, as said below
- send_table: int32 [3, 131072], P(None, ('curve', 'group')), may hold values from 0 to 127, as said below
- recv_table: int32 [4, 131072], P(None, ('curve', 'group')), may hold values from 0 to 127, as said below
Outputs:
- first_image: float32 [5, 64, 131072], P(None, None, ('curve', 'group'))
- second_image: float32 [5, 64, 131072], P(None, None, ('curve', 'group'))
The draws below stay inside these ranges and needn't reach their ends.
Inputs may be any that keep to these rules, and one draw needn't show every extreme that they name: `neighbours`: each entry is -1 (wall), -2 (a fine or coarse face of a mortar slot in use), or the id of the element across the face. Ids are Morton positions; device d holds ids d * 128 to (d + 1) * 128 - 1, and a neighbour id lies at most 64 ids before or after its element's device range; that distance is reached. Across an even face the neighbour id is lower than the element's, across an odd face higher. The neighbour's matching face is f xor 1, with face nodes in the same order. `send_table`: each device's 4 * 32 slots are grouped by destination index in its group, 32 slots each, used slots first. Row 0: local index of the fine element, row 1: its face, row 2: 1 if used, else 0; unused slots hold zeros. A device names each of its (element, face) pairs at most once. In every group one device receives exactly 32 used slots from every device of the group. `recv_table`: each device's slots are grouped by source index in its group, in the sender's slot order. Row 0: local index of the coarse element, row 1: its face, the fine face xor 1, row 2: the child position 0 to 3, row 3: the sender's used flag; unused slots hold zeros.
All inputs are finite; a program needn't handle non-finite values.
Results may differ from the reference program's by a relative error of at most 0.0001.
Values sent between devices are 32-bit elements; how exact they have to be, the bound alone decides.
No kernel may reach another device: no remote copies, remote signals or barrier semaphores. Data moves between devices by JAX's collectives and lax.ppermute only.
A program may use at most 128 MiB of HBM per device.

```python
import math
import jax
import jax.numpy as jnp
import numpy as np
from jax import lax

FIELDS = 5
NODES = 64
ELEM_DEV = 128
CAP = 32
ELEMS = 131072
N_CURVE = 256
N_GROUP = 4
DEVICES = 1024


def mesh_tables(key):
    per_dev = ELEM_DEV
    rim_width = ELEM_DEV // 2
    total = ELEM_DEV * DEVICES
    groups = N_GROUP
    curves = N_CURVE
    capacity = CAP
    subkeys = jax.random.split(key, 9)
    global_ids = jnp.arange(total, dtype=jnp.int32)
    local_ids = global_ids % per_dev
    step_x = 1 + jax.random.randint(subkeys[0], (2, total), 0, 2)
    step_y = 2 + jax.random.randint(subkeys[1], (2, total), 0, rim_width // 4)
    far_step = rim_width - jax.random.randint(subkeys[2], (2, total), 0, rim_width // 2)
    far_step = jnp.stack([jnp.where(local_ids == 0, rim_width, far_step[0]), jnp.where(local_ids == per_dev - 1, rim_width, far_step[1])])
    face_steps = jnp.stack([step_x, step_y, far_step]).reshape(6, total)
    face_signs = jnp.array([-1, 1, -1, 1, -1, 1], dtype=jnp.int32)[:, None]
    linked = global_ids[None, :] + face_signs * face_steps
    wall_mask = jax.random.randint(subkeys[3], (6, total), 0, 16) == 0
    linked = jnp.where((linked < 0) | (linked >= total) | wall_mask, -1, linked).astype(jnp.int32)
    counts = jax.random.randint(subkeys[4], (curves, groups, groups), 1, capacity + 1)
    fullest = jax.random.randint(subkeys[5], (curves,), 0, groups)
    counts = jnp.where(jnp.arange(groups)[None, None, :] == fullest[:, None, None], capacity, counts)
    slot_ids = jnp.arange(capacity, dtype=jnp.int32)
    used_slot = (slot_ids[None, None, None, :] < counts[..., None]).astype(jnp.int32)
    device_keys = jax.random.split(subkeys[6], DEVICES)
    shuffled = jax.vmap(lambda k: jax.random.permutation(k, 6 * per_dev)[:groups * capacity])(device_keys)
    shuffled = shuffled.reshape(curves, groups, groups, capacity).astype(jnp.int32)
    fine_face = shuffled // per_dev * used_slot
    fine_elem = shuffled % per_dev * used_slot
    child = jax.random.randint(subkeys[7], (curves, groups, groups, capacity), 0, 4) * used_slot
    coarse_elem = jax.random.randint(subkeys[8], (curves, groups, groups, capacity), 0, per_dev) * used_slot
    coarse_face = jnp.bitwise_xor(fine_face, 1) * used_slot
    curve_pos = jnp.arange(curves, dtype=jnp.int32)[:, None, None, None]
    source = jnp.arange(groups, dtype=jnp.int32)[None, :, None, None]
    target = jnp.arange(groups, dtype=jnp.int32)[None, None, :, None]
    fine_global = jnp.where(used_slot > 0, (curve_pos * groups + source) * per_dev + fine_elem, total)
    coarse_global = jnp.where(used_slot > 0, (curve_pos * groups + target) * per_dev + coarse_elem, total)
    linked = linked.at[fine_face.reshape(-1), fine_global.reshape(-1)].set(-2, mode='drop')
    linked = linked.at[coarse_face.reshape(-1), coarse_global.reshape(-1)].set(-2, mode='drop')
    send_rows = jnp.stack([fine_elem, fine_face, used_slot]).reshape(3, -1).astype(jnp.int32)
    recv_rows = jnp.swapaxes(jnp.stack([coarse_elem, coarse_face, child, used_slot]), 2, 3).reshape(4, -1).astype(jnp.int32)
    return (linked, send_rows, recv_rows)


def draw_neighbours(key, part):
    return mesh_tables(key)[0]


def draw_send_table(key, part):
    return mesh_tables(key)[1]


def draw_recv_table(key, part):
    return mesh_tables(key)[2]


def shard_levels(own_key, dims, pieces, least, top_value):
    loudness = 1.0
    for position, shards_of in pieces:
        heights = jax.random.uniform(jax.random.fold_in(jax.random.fold_in(own_key, 6), position), (shards_of,), jnp.float32, least / len(pieces), top_value / len(pieces))
        loudness = loudness * jnp.repeat(jnp.exp(heights), dims[position] // shards_of).reshape((-1,) + (1,) * (len(dims) - 1 - position))
    return loudness


def noise(rng, dims, spread, bound, pieces=(), kind=jnp.bfloat16):
    result = jax.random.normal(rng, dims, jnp.float32) * spread
    if len(pieces) > 0:
        result = shard_levels(rng, dims, pieces, -0.22, 0.18) * result
    return jnp.clip(result, min=-bound, max=bound).astype(kind)


def setup_inputs(seed: int = 0) -> dict:
    key_of = jax.random.split(jax.random.key(seed), 7)
    tangent = noise(key_of[0], (FIELDS, NODES, ELEMS), 1.0, 6.0, ((2, 1024),), jnp.float32)
    flux_jacobian = noise(key_of[1], (3, FIELDS, FIELDS, ELEMS), 0.3, 1.75, ((3, 1024),), jnp.float32)
    viscosity = jnp.clip(jnp.exp(math.log(0.2) - 2.3025851 * jax.random.uniform(key_of[2], (ELEMS,), jnp.float32) ** shard_levels(key_of[2], (ELEMS,), ((0, 1024),), -0.2, 0.2)), 0.02, 0.2)
    neighbours = draw_neighbours(jax.random.fold_in(key_of[6], 71), 0)
    send_table = draw_send_table(jax.random.fold_in(key_of[6], 71), 0)
    recv_table = draw_recv_table(jax.random.fold_in(key_of[6], 71), 0)
    return {"tangent": tangent, "flux_jacobian": flux_jacobian, "viscosity": viscosity, "neighbours": neighbours, "send_table": send_table, "recv_table": recv_table}


lift_coef = 6.0
jump_coef = 1.0
pseudo_step = 0.05
highest = lax.Precision.HIGHEST

def node_tables():
    points = np.array([-1.0, -1.0 / np.sqrt(5.0), 1.0 / np.sqrt(5.0), 1.0])
    weights = np.array([1.0, 5.0, 5.0, 1.0]) / 6.0
    barycentric = np.array([1.0 / np.prod([points[j] - points[k] for k in range(4) if k != j]) for j in range(4)])
    derivative = np.zeros((4, 4))
    for a in range(4):
        for b in range(4):
            if a != b:
                derivative[a, b] = barycentric[b] / barycentric[a] / (points[a] - points[b])
        derivative[a, a] = -np.sum(derivative[a])
    halves = []
    for upper_half in range(2):
        matrix = np.zeros((4, 4))
        for a in range(4):
            target = 0.5 * points[a] + upper_half - 0.5
            for b in range(4):
                matrix[a, b] = np.prod([(target - points[k]) / (points[b] - points[k]) for k in range(4) if k != b])
        halves.append(matrix)
    surface_weights = np.kron(weights, weights)
    interpolate = np.stack([np.kron(halves[c // 2], halves[c % 2]) for c in range(4)])
    project = np.stack([0.25 * (interpolate[c].T * surface_weights[None, :]) / surface_weights[:, None] for c in range(4)])
    return (jnp.asarray(derivative, jnp.float32), jnp.asarray(interpolate, jnp.float32), jnp.asarray(project, jnp.float32))

def derive(nodal_field, direction, derivative):
    forms = ('ab,fkjbe->fkjae', 'ab,fkbie->fkaie', 'ab,fbjie->fajie')
    return jnp.einsum(forms[direction], derivative, nodal_field, precision=highest)

def flux_of(jacobian, nodal_field, direction):
    running = jacobian[direction, :, 0][:, None, None, None, :] * nodal_field[0][None]
    for b in range(1, 5):
        running = running + jacobian[direction, :, b][:, None, None, None, :] * nodal_field[b][None]
    return running

def face_of(nodal_field, face):
    return jnp.take(nodal_field, 3 * (face % 2), axis=3 - face // 2).reshape(5, 16, nodal_field.shape[-1])

def add_face(nodal_field, face, values):
    slicer = [slice(None)] * 5
    slicer[3 - face // 2] = 3 * (face % 2)
    return nodal_field.at[tuple(slicer)].add(values.reshape(5, 4, 4, values.shape[-1]))

def local_terms(vector, jacobian, viscosity, derivative):
    elements = vector.shape[-1]
    nodal_field = vector.reshape(5, 4, 4, 4, elements)
    fluxes = [flux_of(jacobian, nodal_field, d) for d in range(3)]
    volume = jnp.zeros_like(nodal_field)
    for d in range(3):
        second_der = derive(derive(nodal_field, d, derivative), d, derivative)
        volume = volume - derive(fluxes[d], d, derivative) + viscosity * second_der
    traces_q = jnp.stack([face_of(fluxes[f // 2], f) for f in range(6)])
    traces_w = jnp.stack([face_of(nodal_field, f) for f in range(6)])
    return (volume, traces_q, traces_w)

def face_flux(own_q, own_w, far_q, far_w):
    return 0.5 * (own_q + far_q) + 0.5 * jump_coef * (own_w - far_w)

def select_faces(traces, faces, columns):
    gathered = jnp.take(traces.reshape(6, 80, traces.shape[-1]), columns, axis=2)
    chosen = (faces[None, :] == jnp.arange(6, dtype=jnp.int32)[:, None]).astype(jnp.float32)
    return lax.optimization_barrier(jnp.sum(gathered * chosen[:, None, :], axis=0))

def by_child(values, child, child_tables):
    all_children = jnp.einsum('cpq,fqs->cfps', child_tables, values.reshape(5, 16, -1), precision=highest)
    chosen = (child[None, :] == jnp.arange(4, dtype=jnp.int32)[:, None]).astype(jnp.float32)
    return lax.optimization_barrier(jnp.sum(all_children * chosen[:, None, None, :], axis=0)).reshape(80, -1)

def mortar_terms(fine_q, fine_w, coarse_elem, coarse_face, child, coarse_used, traces_q, traces_w, interpolate, project):
    coarse_sign = (2 * (coarse_face % 2) - 1).astype(jnp.float32)
    coarse_q = coarse_sign * select_faces(traces_q, coarse_face, coarse_elem)
    coarse_w = select_faces(traces_w, coarse_face, coarse_elem)
    inter_q = by_child(coarse_q, child, interpolate)
    inter_w = by_child(coarse_w, child, interpolate)
    fluxes = face_flux(fine_q, fine_w, -inter_q, inter_w)
    coarse_term = -lift_coef * by_child(-fluxes - inter_q, child, project) * coarse_used
    return (fluxes, coarse_term)

def scatter_faces(surface, faces, columns, values):
    chosen = (faces[None, :] == jnp.arange(6, dtype=jnp.int32)[:, None]).astype(jnp.float32)
    return surface.at[:, :, columns].add(chosen[:, None, :] * values[None])

def apply_once(vector, jacobian, viscosity, neighbours, mortar, tables):
    derivative, interpolate, project = tables
    elements = vector.shape[-1]
    volume, traces_q, traces_w = local_terms(vector, jacobian, viscosity, derivative)
    face_terms = []
    for f in range(6):
        normal = 2.0 * (f % 2) - 1.0
        linked_ids = neighbours[f]
        columns = jnp.clip(linked_ids, 0, elements - 1)
        linked = (linked_ids >= 0).astype(jnp.float32)
        far_q = normal * jnp.take(traces_q[f ^ 1], columns, axis=2) * linked
        far_w = jnp.take(traces_w[f ^ 1], columns, axis=2) * linked
        own_q = normal * traces_q[f]
        fluxes = face_flux(own_q, traces_w[f], far_q, far_w)
        face_terms.append(-lift_coef * (fluxes - own_q) * (linked_ids != -2).astype(jnp.float32))
    surface = jnp.stack(face_terms).reshape(6, 80, elements)
    fine_elem, fine_face, fine_used, coarse_elem, coarse_face, child, coarse_used = mortar
    fine_sign = (2 * (fine_face % 2) - 1).astype(jnp.float32)
    fine_q = fine_sign * select_faces(traces_q, fine_face, fine_elem)
    fine_w = select_faces(traces_w, fine_face, fine_elem)
    fluxes, coarse_term = mortar_terms(fine_q, fine_w, coarse_elem, coarse_face, child, coarse_used, traces_q, traces_w, interpolate, project)
    fine_term = -lift_coef * (fluxes - fine_q) * fine_used
    surface = scatter_faces(surface, coarse_face, coarse_elem, coarse_term)
    surface = scatter_faces(surface, fine_face, fine_elem, fine_term)
    residual = volume
    for f in range(6):
        residual = add_face(residual, f, surface[f].reshape(5, 16, elements))
    return vector - pseudo_step * residual.reshape(5, 64, elements)

def reference(tangent, flux_jacobian, viscosity, neighbours, send_table, recv_table):
    tables = node_tables()
    sent_rows = send_table.reshape(3, N_CURVE, N_GROUP, N_GROUP, CAP)
    taken_rows = jnp.swapaxes(recv_table.reshape(4, N_CURVE, N_GROUP, N_GROUP, CAP), 2, 3)
    curve_pos = jnp.arange(N_CURVE, dtype=jnp.int32)[:, None, None, None]
    source = jnp.arange(N_GROUP, dtype=jnp.int32)[None, :, None, None]
    target = jnp.arange(N_GROUP, dtype=jnp.int32)[None, None, :, None]
    fine_global = ((curve_pos * N_GROUP + source) * ELEM_DEV + sent_rows[0]).reshape(-1).astype(jnp.int32)
    coarse_global = ((curve_pos * N_GROUP + target) * ELEM_DEV + taken_rows[0]).reshape(-1).astype(jnp.int32)
    mortar = (fine_global, sent_rows[1].reshape(-1), sent_rows[2].reshape(-1).astype(jnp.float32), coarse_global, taken_rows[1].reshape(-1), taken_rows[2].reshape(-1), taken_rows[3].reshape(-1).astype(jnp.float32))
    first_image = apply_once(tangent, flux_jacobian, viscosity, neighbours, mortar, tables)
    second_image = apply_once(first_image, flux_jacobian, viscosity, neighbours, mortar, tables)
    return (first_image, second_image)
```

```python
import functools

import jax
import jax.numpy as jnp
import ml_dtypes
import numpy as np
from jax import lax
from jax.experimental import pallas as pl
from jax.experimental.pallas import tpu as pltpu
from jax.sharding import PartitionSpec as P

F32 = jnp.float32
BF16 = jnp.bfloat16
AXES = ("curve", "group")
PSEUDO_STEP = 0.05
FACE_SCALE = 0.15


def node_tables():
    points = np.array([-1.0, -1.0 / np.sqrt(5.0), 1.0 / np.sqrt(5.0), 1.0])
    weights = np.array([1.0, 5.0, 5.0, 1.0]) / 6.0
    barycentric = np.array(
        [1.0 / np.prod([points[j] - points[k] for k in range(4) if k != j]) for j in range(4)]
    )
    derivative = np.zeros((4, 4))
    for a in range(4):
        for b in range(4):
            if a != b:
                derivative[a, b] = barycentric[b] / barycentric[a] / (points[a] - points[b])
        derivative[a, a] = -np.sum(derivative[a])
    halves = []
    for upper_half in range(2):
        matrix = np.zeros((4, 4))
        for a in range(4):
            target = 0.5 * points[a] + upper_half - 0.5
            for b in range(4):
                matrix[a, b] = np.prod(
                    [(target - points[k]) / (points[b] - points[k]) for k in range(4) if k != b]
                )
        halves.append(matrix)
    surface_weights = np.kron(weights, weights)
    interpolate = np.stack([np.kron(halves[c // 2], halves[c % 2]) for c in range(4)])
    project = np.stack(
        [
            0.25 * (interpolate[c].T * surface_weights[None, :]) / surface_weights[:, None]
            for c in range(4)
        ]
    )
    return derivative, interpolate, project


def pieces_of(matrix):
    hi = matrix.astype(ml_dtypes.bfloat16)
    lo = (matrix - hi.astype(np.float64)).astype(ml_dtypes.bfloat16)
    return np.concatenate([hi, hi, lo], axis=1)


def operator_tables():
    derivative, interpolate, project = node_tables()
    eye = np.eye(4)
    d_x = np.kron(eye, np.kron(eye, derivative))
    d_y = np.kron(eye, np.kron(derivative, eye))
    d_z = np.kron(derivative, np.kron(eye, eye))
    laplacian = d_x @ d_x + d_y @ d_y + d_z @ d_z
    volume = pieces_of(np.concatenate([d_x, d_y, d_z, laplacian], axis=0))
    return (
        volume,
        pieces_of(interpolate.reshape(64, 16)),
        pieces_of(project.reshape(64, 16)),
    )


def split(x):
    hi = x.astype(BF16)
    lo = (x - hi.astype(F32)).astype(BF16)
    return hi, lo


def dot(a, b):
    return lax.dot_general(a, b, (((1,), (0,)), ((), ())), preferred_element_type=F32)


def one_hot(index, rows):
    place = lax.broadcasted_iota(jnp.int32, (rows, index.shape[1]), 0)
    return jnp.where(place == index, 1.0, 0.0).astype(BF16)


def slot_one_hots(send_ref, recv_ref):
    fine = jnp.where(send_ref[2:3, :] > 0, send_ref[1:2, :] * 128 + send_ref[0:1, :], -1)
    coarse = jnp.where(recv_ref[3:4, :] > 0, recv_ref[1:2, :] * 128 + recv_ref[0:1, :], -1)
    return jnp.concatenate([one_hot(fine, 768), one_hot(coarse, 768)], axis=1)


def by_child(table_ref, values, recv_ref):
    count = len(values)
    hi, lo = split(jnp.concatenate(values, axis=1))
    product = dot(table_ref[...], jnp.concatenate([hi, lo, hi], axis=0))
    child = recv_ref[2:3, :]
    picks = [jnp.where(child == c, 1.0, 0.0) for c in range(4)]
    return [
        sum(
            product[16 * c : 16 * c + 16, 128 * n : 128 * n + 128] * picks[c]
            for c in range(4)
        )
        for n in range(count)
    ]


def face_values(v_ref, face, a):
    d, s = face // 2, face % 2
    if d == 0:
        return v_ref[a, pl.ds(3 * s, 16, stride=4), :]
    if d == 1:
        return jnp.concatenate(
            [v_ref[a, 16 * k + 12 * s : 16 * k + 12 * s + 4, :] for k in range(4)], axis=0
        )
    return v_ref[a, 48 * s : 48 * s + 16, :]


def add_to_face(o_ref, face, a, values):
    d, s = face // 2, face % 2
    if d == 0:
        o_ref[a, pl.ds(3 * s, 16, stride=4), :] += values
    elif d == 1:
        for k in range(4):
            row = 16 * k + 12 * s
            o_ref[a, row : row + 4, :] += values[4 * k : 4 * k + 4]
    else:
        o_ref[a, 48 * s : 48 * s + 16, :] += values


def trace_part(v_ref, j_ref, send_ref, recv_ref, it_ref, g_ref, loc_ref, up_ref, down_ref, m_ref):
    gs, hs = [], []
    for f in range(6):
        normal = 2.0 * (f % 2) - 1.0
        w = [face_values(v_ref, f, b) for b in range(5)]
        g_rows, h_rows = [], []
        for a in range(5):
            q = j_ref[f // 2, a, 0:1, :] * w[0]
            for b in range(1, 5):
                q = q + j_ref[f // 2, a, b : b + 1, :] * w[b]
            q = normal * q
            g_rows.append(w[a] + q)
            h_rows.append(w[a] - q)
        gs.append(jnp.concatenate(g_rows, axis=0))
        hs.append(jnp.concatenate(h_rows, axis=0))
        g_ref[f] = gs[f]
    lane = lax.broadcasted_iota(jnp.int32, (120, 128), 1)
    odd = jnp.concatenate([gs[1], gs[3], gs[5]], axis=0)
    even = jnp.concatenate([gs[0], gs[2], gs[4]], axis=0)
    up_ref[...] = jnp.where(lane < 64, pltpu.roll(odd[:120], 64, 1), odd[120:])
    down_ref[...] = jnp.where(lane < 64, even[:120], pltpu.roll(even[120:], 64, 1))
    hots = slot_one_hots(send_ref, recv_ref)
    g_hi, g_lo = split(jnp.concatenate(gs, axis=1))
    h_hi, h_lo = split(jnp.concatenate(hs, axis=1))
    picked = dot(jnp.concatenate([g_hi, g_lo, h_hi, h_lo], axis=0), hots)
    g_slots = picked[0:80] + picked[80:160]
    h_slots = picked[160:240] + picked[240:320]
    g_fine, g_coarse = g_slots[:, :128], g_slots[:, 128:]
    h_fine, h_coarse = h_slots[:, :128], h_slots[:, 128:]
    rows = [g_coarse[16 * a : 16 * a + 16] for a in range(5)]
    rows += [h_coarse[16 * a : 16 * a + 16] for a in range(5)]
    inter = by_child(it_ref, rows, recv_ref)
    g_inter = jnp.concatenate(inter[:5], axis=0)
    h_inter = jnp.concatenate(inter[5:], axis=0)
    loc_ref[...] = jnp.concatenate([h_inter, h_fine], axis=0)
    outgoing = jnp.concatenate([g_fine, g_inter], axis=0)
    quarter = lax.broadcasted_iota(jnp.int32, (40, 128), 1) // 32
    for t in range(4):
        block = None
        for q in range(4):
            part = outgoing[40 * q : 40 * q + 40]
            shift = (32 * (q - t)) % 128
            part = pltpu.roll(part, shift, 1) if shift else part
            block = part if block is None else jnp.where(quarter == q, part, block)
        m_ref[t] = block


def combine_part(
    base_ref, g_ref, loc_ref, before_ref, after_ref, m_ref, nb_ref, send_ref, recv_ref, pt_ref, o_ref
):
    first_id = (lax.axis_index("curve") * 4 + lax.axis_index("group")) * 128
    o_ref[...] = base_ref[...]
    quarter = lax.broadcasted_iota(jnp.int32, (40, 128), 1) // 32
    parts = []
    for q in range(4):
        part = None
        for s in range(4):
            shift = (32 * (s - q)) % 128
            block = m_ref[s]
            block = pltpu.roll(block, shift, 1) if shift else block
            part = block if part is None else jnp.where(quarter == s, block, part)
        parts.append(part)
    incoming = jnp.concatenate(parts, axis=0) - loc_ref[...]
    projected = by_child(pt_ref, [incoming[16 * a : 16 * a + 16] for a in range(5)], recv_ref)
    values = jnp.concatenate([incoming[80:160], jnp.concatenate(projected, axis=0)], axis=1)
    hi, lo = split(values)
    hots = slot_one_hots(send_ref, recv_ref)
    spread = lax.dot_general(
        jnp.concatenate([hi, lo], axis=0),
        hots,
        (((1,), (1,)), ((), ())),
        preferred_element_type=F32,
    )
    mortar = spread[0:80] + spread[80:160]
    before, after = before_ref[...], after_ref[...]
    before = jnp.concatenate([before, pltpu.roll(before, 64, 1)], axis=0)
    after = jnp.concatenate([after, pltpu.roll(after, 64, 1)], axis=0)
    for f in range(6):
        linked = nb_ref[f : f + 1, :]
        place = linked - first_id
        if f % 2 == 0:
            halo = before
            place = jnp.where(place < 0, place + 192, place)
        else:
            halo = after
        place = jnp.where(linked < 0, -1, place)
        third = f // 2
        source = jnp.concatenate([g_ref[f ^ 1], halo[80 * third : 80 * third + 80]], axis=1)
        hi, lo = split(source)
        far = dot(jnp.concatenate([hi, lo], axis=0), one_hot(place, 256))
        total = far[0:80] + far[80:160] + mortar[:, 128 * f : 128 * f + 128]
        total = total * (-FACE_SCALE)
        for a in range(5):
            add_to_face(o_ref, f, a, total[16 * a : 16 * a + 16])


def trace_kernel(v_ref, j_ref, send_ref, recv_ref, it_ref, g_ref, loc_ref, up_ref, down_ref, m_ref):
    trace_part(v_ref, j_ref, send_ref, recv_ref, it_ref, g_ref, loc_ref, up_ref, down_ref, m_ref)


def volume_kernel(v_ref, j_ref, visc_ref, nb_ref, g_ref, vt_ref, o_ref):
    v = v_ref[...]
    hi, lo = split(jnp.concatenate([v[a] for a in range(5)], axis=1))
    terms = dot(vt_ref[...], jnp.concatenate([hi, lo, hi], axis=0))
    visc = visc_ref[...].reshape(1, 128)
    for a in range(5):
        total = visc * terms[192:256, 128 * a : 128 * a + 128]
        for d in range(3):
            for b in range(5):
                total = total - j_ref[d, a, b : b + 1, :] * terms[
                    64 * d : 64 * d + 64, 128 * b : 128 * b + 128
                ]
        o_ref[a] = v[a] - PSEUDO_STEP * total
    for f in range(6):
        mask = jnp.where(nb_ref[f : f + 1, :] != -2, FACE_SCALE, 0.0)
        for a in range(5):
            h = 2.0 * face_values(v_ref, f, a) - g_ref[f, 16 * a : 16 * a + 16, :]
            add_to_face(o_ref, f, a, mask * h)


def middle_kernel(
    base_ref, g_ref, loc_ref, before_ref, after_ref, m_ref, nb_ref, send_ref, recv_ref,
    j_ref, it_ref, pt_ref,
    o_ref, g2_ref, loc2_ref, up_ref, down_ref, m2_ref,
):
    combine_part(
        base_ref, g_ref, loc_ref, before_ref, after_ref, m_ref, nb_ref, send_ref, recv_ref, pt_ref, o_ref
    )
    trace_part(o_ref, j_ref, send_ref, recv_ref, it_ref, g2_ref, loc2_ref, up_ref, down_ref, m2_ref)


def final_kernel(
    base_ref, g_ref, loc_ref, before_ref, after_ref, m_ref, nb_ref, send_ref, recv_ref, pt_ref, o_ref
):
    combine_part(
        base_ref, g_ref, loc_ref, before_ref, after_ref, m_ref, nb_ref, send_ref, recv_ref, pt_ref, o_ref
    )


def shape(*dims):
    return jax.ShapeDtypeStruct(dims, F32)


def call(kernel, outs, *args):
    return pl.pallas_call(
        kernel,
        out_shape=outs,
        compiler_params=pltpu.CompilerParams(vmem_limit_bytes=32 * 1024 * 1024),
    )(*args)


IMAGE = (5, 64, 128)
TRACES = (shape(6, 80, 128), shape(160, 128), shape(120, 128), shape(120, 128), shape(4, 40, 128))


def exchange(up, down, mortar):
    count = lax.axis_size(AXES)
    onward = [(i, i + 1) for i in range(count - 1)]
    back = [(i + 1, i) for i in range(count - 1)]
    mortar = lax.all_to_all(mortar, "group", split_axis=0, concat_axis=0, tiled=True)
    before = lax.ppermute(up, AXES, onward)
    after = lax.ppermute(down, AXES, back)
    return before, after, mortar


def local(tangent, jacobian, viscosity, neighbours, send_table, recv_table):
    volume_table, inter_table, project_table = (jnp.asarray(t) for t in operator_tables())
    g, loc, up, down, mortar = call(
        trace_kernel, TRACES, tangent, jacobian, send_table, recv_table, inter_table
    )
    before, after, mortar = exchange(up, down, mortar)
    base = call(
        volume_kernel, shape(*IMAGE), tangent, jacobian, viscosity, neighbours, g, volume_table
    )
    first, g, loc, up, down, mortar = call(
        middle_kernel,
        (shape(*IMAGE),) + TRACES,
        base, g, loc, before, after, mortar, neighbours, send_table, recv_table,
        jacobian, inter_table, project_table,
    )
    before, after, mortar = exchange(up, down, mortar)
    base = call(
        volume_kernel, shape(*IMAGE), first, jacobian, viscosity, neighbours, g, volume_table
    )
    second = call(
        final_kernel,
        shape(*IMAGE),
        base, g, loc, before, after, mortar, neighbours, send_table, recv_table, project_table,
    )
    return first, second


def solution(mesh):
    in_specs = (
        P(None, None, AXES),
        P(None, None, None, AXES),
        P(AXES),
        P(None, AXES),
        P(None, AXES),
        P(None, AXES),
    )
    out_specs = (P(None, None, AXES), P(None, None, AXES))
    return jax.shard_map(local, mesh=mesh, in_specs=in_specs, out_specs=out_specs, check_vma=False)
```

```python
import jax
import jax.numpy as jnp
import ml_dtypes
import numpy as np
from jax import lax
from jax.experimental import pallas as pl
from jax.experimental.pallas import tpu as pltpu
from jax.sharding import PartitionSpec as P

F32 = jnp.float32
BF16 = jnp.bfloat16
AXES = ("curve", "group")
PSEUDO_STEP = 0.05
FACE_SCALE = 0.15


def node_tables():
    points = np.array([-1.0, -1.0 / np.sqrt(5.0), 1.0 / np.sqrt(5.0), 1.0])
    weights = np.array([1.0, 5.0, 5.0, 1.0]) / 6.0
    barycentric = np.array(
        [1.0 / np.prod([points[j] - points[k] for k in range(4) if k != j]) for j in range(4)]
    )
    derivative = np.zeros((4, 4))
    for a in range(4):
        for b in range(4):
            if a != b:
                derivative[a, b] = barycentric[b] / barycentric[a] / (points[a] - points[b])
        derivative[a, a] = -np.sum(derivative[a])
    halves = []
    for upper_half in range(2):
        matrix = np.zeros((4, 4))
        for a in range(4):
            target = 0.5 * points[a] + upper_half - 0.5
            for b in range(4):
                matrix[a, b] = np.prod(
                    [(target - points[k]) / (points[b] - points[k]) for k in range(4) if k != b]
                )
        halves.append(matrix)
    surface_weights = np.kron(weights, weights)
    interpolate = np.stack([np.kron(halves[c // 2], halves[c % 2]) for c in range(4)])
    project = np.stack(
        [
            0.25 * (interpolate[c].T * surface_weights[None, :]) / surface_weights[:, None]
            for c in range(4)
        ]
    )
    return derivative, interpolate, project


def pieces_of(matrix):
    hi = matrix.astype(ml_dtypes.bfloat16)
    lo = (matrix - hi.astype(np.float64)).astype(ml_dtypes.bfloat16)
    return np.concatenate([hi, hi, lo], axis=1)


def operator_tables():
    derivative, interpolate, project = node_tables()
    eye = np.eye(4)
    d_x = np.kron(eye, np.kron(eye, derivative))
    d_y = np.kron(eye, np.kron(derivative, eye))
    d_z = np.kron(derivative, np.kron(eye, eye))
    laplacian = d_x @ d_x + d_y @ d_y + d_z @ d_z
    volume = pieces_of(np.concatenate([d_x, d_y, d_z, laplacian], axis=0))
    return (
        volume,
        pieces_of(interpolate.reshape(64, 16)),
        pieces_of(project.reshape(64, 16)),
    )


def split(x):
    hi = x.astype(BF16)
    lo = (x - hi.astype(F32)).astype(BF16)
    return hi, lo


def dot(a, b):
    return lax.dot_general(a, b, (((1,), (0,)), ((), ())), preferred_element_type=F32)


def one_hot(index, rows):
    place = lax.broadcasted_iota(jnp.int32, (rows, index.shape[1]), 0)
    return jnp.where(place == index, 1.0, 0.0).astype(BF16)


def slot_one_hots(send_ref, recv_ref):
    fine = jnp.where(send_ref[2:3, :] > 0, send_ref[1:2, :] * 128 + send_ref[0:1, :], -1)
    coarse = jnp.where(recv_ref[3:4, :] > 0, recv_ref[1:2, :] * 128 + recv_ref[0:1, :], -1)
    return jnp.concatenate([one_hot(fine, 768), one_hot(coarse, 768)], axis=1)


def by_child(table_ref, values, recv_ref):
    count = len(values)
    hi, lo = split(jnp.concatenate(values, axis=1))
    product = dot(table_ref[...], jnp.concatenate([hi, lo, hi], axis=0))
    child = recv_ref[2:3, :]
    picks = [jnp.where(child == c, 1.0, 0.0) for c in range(4)]
    return [
        sum(
            product[16 * c : 16 * c + 16, 128 * n : 128 * n + 128] * picks[c]
            for c in range(4)
        )
        for n in range(count)
    ]


def face_values(v_ref, face, a):
    d, s = face // 2, face % 2
    if d == 0:
        return v_ref[a, pl.ds(3 * s, 16, stride=4), :]
    if d == 1:
        return jnp.concatenate(
            [v_ref[a, 16 * k + 12 * s : 16 * k + 12 * s + 4, :] for k in range(4)], axis=0
        )
    return v_ref[a, 48 * s : 48 * s + 16, :]


def add_to_face(o_ref, face, a, values):
    d, s = face // 2, face % 2
    if d == 0:
        o_ref[a, pl.ds(3 * s, 16, stride=4), :] += values
    elif d == 1:
        for k in range(4):
            row = 16 * k + 12 * s
            o_ref[a, row : row + 4, :] += values[4 * k : 4 * k + 4]
    else:
        o_ref[a, 48 * s : 48 * s + 16, :] += values


def trace_part(v_ref, j_ref, g_ref, edge_ref):
    for f in range(6):
        d = f // 2
        w = [face_values(v_ref, f, b) for b in range(5)]
        for a in range(5):
            q = j_ref[a, 0, d : d + 1, :] * w[0]
            for b in range(1, 5):
                q = q + j_ref[a, b, d : d + 1, :] * w[b]
            g_ref[f, 16 * a : 16 * a + 16, :] = w[a] + q if f % 2 else w[a] - q
    up, down = rims(g_ref)
    edge_ref[...] = jnp.where(lax.axis_index("group") == 0, down, up)


def rims(g_ref):
    odd = jnp.concatenate([g_ref[1], g_ref[3], g_ref[5]], axis=0)
    even = jnp.concatenate([g_ref[0], g_ref[2], g_ref[4]], axis=0)
    lane = lax.broadcasted_iota(jnp.int32, (120, 128), 1)
    up = jnp.where(lane < 64, pltpu.roll(odd[:120], 64, 1), odd[120:])
    down = jnp.where(lane < 64, even[:120], pltpu.roll(even[120:], 64, 1))
    return up, down


def mortar_part(v_ref, g_ref, hots, recv_ref, it_ref, loc_ref, m_ref):
    gs = [g_ref[f] for f in range(6)]
    ws = [
        jnp.concatenate([face_values(v_ref, f, a) for a in range(5)], axis=0) for f in range(6)
    ]
    hs = [2.0 * ws[f] - gs[f] for f in range(6)]
    g_hi, g_lo = split(jnp.concatenate(gs, axis=1))
    h_hi, h_lo = split(jnp.concatenate(hs, axis=1))
    picked = dot(jnp.concatenate([g_hi, g_lo, h_hi, h_lo], axis=0), hots)
    g_slots = picked[0:80] + picked[80:160]
    h_slots = picked[160:240] + picked[240:320]
    g_fine, g_coarse = g_slots[:, :128], g_slots[:, 128:]
    h_fine, h_coarse = h_slots[:, :128], h_slots[:, 128:]
    rows = [g_coarse[16 * a : 16 * a + 16] for a in range(5)]
    rows += [h_coarse[16 * a : 16 * a + 16] for a in range(5)]
    inter = by_child(it_ref, rows, recv_ref)
    g_inter = jnp.concatenate(inter[:5], axis=0)
    h_inter = jnp.concatenate(inter[5:], axis=0)
    loc_ref[...] = jnp.concatenate([h_inter, h_fine], axis=0)
    outgoing = jnp.concatenate([g_fine, g_inter], axis=0)
    quarter = lax.broadcasted_iota(jnp.int32, (40, 128), 1) // 32
    up, down = rims(g_ref)
    me = lax.axis_index("group")
    for t in range(4):
        block = None
        for q in range(4):
            part = outgoing[40 * q : 40 * q + 40]
            shift = (32 * (q - t)) % 128
            part = pltpu.roll(part, shift, 1) if shift else part
            block = part if block is None else jnp.where(quarter == q, part, block)
        m_ref[t, 0:40, :] = block
        m_ref[t, 40:160, :] = jnp.where(me < t, up, down)


def conforming_one_hots(nb_ref, hot_ref):
    first_id = (lax.axis_index("curve") * 4 + lax.axis_index("group")) * 128
    for f in range(6):
        linked = nb_ref[f : f + 1, :]
        place = linked - first_id
        if f % 2 == 0:
            place = jnp.where(place < 0, place + 192, place)
        hot_ref[f] = one_hot(jnp.where(linked < 0, -1, place), 256)


def combine_part(base_ref, g_ref, loc_ref, edge_ref, m_ref, hot_ref, slot_ref, recv_ref, pt_ref, o_ref):
    me = lax.axis_index("group")
    o_ref[...] = base_ref[...]
    edge = edge_ref[...]
    before = jnp.where(me == 0, edge, m_ref[jnp.maximum(me - 1, 0), 40:160, :])
    after = jnp.where(me == 3, edge, m_ref[jnp.minimum(me + 1, 3), 40:160, :])
    quarter = lax.broadcasted_iota(jnp.int32, (40, 128), 1) // 32
    parts = []
    for q in range(4):
        part = None
        for s in range(4):
            shift = (32 * (s - q)) % 128
            block = m_ref[s, 0:40, :]
            block = pltpu.roll(block, shift, 1) if shift else block
            part = block if part is None else jnp.where(quarter == s, block, part)
        parts.append(part)
    incoming = jnp.concatenate(parts, axis=0) - loc_ref[...]
    projected = by_child(pt_ref, [incoming[16 * a : 16 * a + 16] for a in range(5)], recv_ref)
    values = jnp.concatenate([incoming[80:160], jnp.concatenate(projected, axis=0)], axis=1)
    hi, lo = split(values)
    spread = lax.dot_general(
        jnp.concatenate([hi, lo], axis=0),
        slot_ref[...],
        (((1,), (1,)), ((), ())),
        preferred_element_type=F32,
    )
    mortar = spread[0:80] + spread[80:160]
    before = jnp.concatenate([before, pltpu.roll(before, 64, 1)], axis=0)
    after = jnp.concatenate([after, pltpu.roll(after, 64, 1)], axis=0)
    for f in range(6):
        halo = after if f % 2 else before
        third = f // 2
        source = jnp.concatenate([g_ref[f ^ 1], halo[80 * third : 80 * third + 80]], axis=1)
        hi, lo = split(source)
        far = dot(jnp.concatenate([hi, lo], axis=0), hot_ref[f])
        total = far[0:80] + far[80:160] + mortar[:, 128 * f : 128 * f + 128]
        total = total * (-FACE_SCALE)
        for a in range(5):
            add_to_face(o_ref, f, a, total[16 * a : 16 * a + 16])


def volume_part(v_ref, j_ref, visc_ref, nb_ref, g_ref, vt_ref, o_ref):
    v = v_ref[...]
    hi, lo = split(jnp.concatenate([v[a] for a in range(5)], axis=1))
    terms = dot(vt_ref[...], jnp.concatenate([hi, lo, hi], axis=0))
    visc = visc_ref[...].reshape(1, 128)
    for a in range(5):
        total = visc * terms[192:256, 128 * a : 128 * a + 128]
        for d in range(3):
            for b in range(5):
                total = total - j_ref[a, b, d : d + 1, :] * terms[
                    64 * d : 64 * d + 64, 128 * b : 128 * b + 128
                ]
        o_ref[a] = v[a] - PSEUDO_STEP * total
    for f in range(6):
        mask = jnp.where(nb_ref[f : f + 1, :] != -2, FACE_SCALE, 0.0)
        for a in range(5):
            h = 2.0 * face_values(v_ref, f, a) - g_ref[f, 16 * a : 16 * a + 16, :]
            add_to_face(o_ref, f, a, mask * h)


def first_traces(v_ref, j_ref, g_ref, edge_ref):
    trace_part(v_ref, j_ref, g_ref, edge_ref)


def first_mortars(v_ref, g_ref, send_ref, recv_ref, it_ref, loc_ref, m_ref, slot_ref):
    hots = slot_one_hots(send_ref, recv_ref)
    slot_ref[...] = hots
    mortar_part(v_ref, g_ref, hots, recv_ref, it_ref, loc_ref, m_ref)


def second_mortars(v_ref, g_ref, slot_ref, recv_ref, it_ref, loc_ref, m_ref):
    mortar_part(v_ref, g_ref, slot_ref[...], recv_ref, it_ref, loc_ref, m_ref)


def first_volume(v_ref, j_ref, visc_ref, nb_ref, g_ref, vt_ref, o_ref, hot_ref):
    volume_part(v_ref, j_ref, visc_ref, nb_ref, g_ref, vt_ref, o_ref)
    conforming_one_hots(nb_ref, hot_ref)


def second_volume(v_ref, j_ref, visc_ref, nb_ref, g_ref, vt_ref, o_ref):
    volume_part(v_ref, j_ref, visc_ref, nb_ref, g_ref, vt_ref, o_ref)


def middle(
    base_ref, g_ref, loc_ref, edge_ref, m_ref, hot_ref, slot_ref, recv_ref, pt_ref, j_ref,
    o_ref, g2_ref, edge2_ref,
):
    combine_part(base_ref, g_ref, loc_ref, edge_ref, m_ref, hot_ref, slot_ref, recv_ref, pt_ref, o_ref)
    trace_part(o_ref, j_ref, g2_ref, edge2_ref)


def shape(*dims, kind=F32):
    return jax.ShapeDtypeStruct(dims, kind)


def call(kernel, outs, *args):
    return pl.pallas_call(
        kernel,
        out_shape=outs,
        compiler_params=pltpu.CompilerParams(vmem_limit_bytes=32 * 1024 * 1024),
    )(*args)


IMAGE = shape(5, 64, 128)
TRACES = shape(6, 80, 128)
EDGE = shape(120, 128)
SLOTS = shape(160, 128)
MESSAGE = shape(4, 160, 128)
SLOT_HOTS = shape(768, 256, kind=BF16)
FACE_HOTS = shape(6, 256, 128, kind=BF16)


def swap_edges(edge):
    ends = [(4 * c + 3, 4 * c + 4) for c in range(lax.axis_size("curve") - 1)]
    return lax.ppermute(edge, AXES, ends + [(j, i) for i, j in ends])


def exchange(message):
    return lax.all_to_all(message, "group", split_axis=0, concat_axis=0, tiled=True)


def local(tangent, jacobian, viscosity, neighbours, send_table, recv_table):
    volume_table, inter_table, project_table = (jnp.asarray(t) for t in operator_tables())
    jacobian = jnp.transpose(jacobian, (1, 2, 0, 3))
    g, edge = call(first_traces, (TRACES, EDGE), tangent, jacobian)
    edge = swap_edges(edge)
    loc, message, slots = call(
        first_mortars, (SLOTS, MESSAGE, SLOT_HOTS), tangent, g, send_table, recv_table, inter_table
    )
    message = exchange(message)
    base, hots = call(
        first_volume,
        (IMAGE, FACE_HOTS),
        tangent, jacobian, viscosity, neighbours, g, volume_table,
    )
    first, g, edge = call(
        middle,
        (IMAGE, TRACES, EDGE),
        base, g, loc, edge, message, hots, slots, recv_table, project_table, jacobian,
    )
    edge = swap_edges(edge)
    loc, message = call(
        second_mortars, (SLOTS, MESSAGE), first, g, slots, recv_table, inter_table
    )
    message = exchange(message)
    base = call(
        second_volume, IMAGE, first, jacobian, viscosity, neighbours, g, volume_table
    )
    second = call(
        combine_part,
        IMAGE,
        base, g, loc, edge, message, hots, slots, recv_table, project_table,
    )
    return first, second


def solution(mesh):
    in_specs = (
        P(None, None, AXES),
        P(None, None, None, AXES),
        P(AXES),
        P(None, AXES),
        P(None, AXES),
        P(None, AXES),
    )
    out_specs = (P(None, None, AXES), P(None, None, AXES))
    return jax.shard_map(local, mesh=mesh, in_specs=in_specs, out_specs=out_specs, check_vma=False)
```

```python
import jax
import jax.numpy as jnp
import ml_dtypes
import numpy as np
from jax import lax
from jax.experimental import pallas as pl
from jax.experimental.pallas import tpu as pltpu
from jax.sharding import PartitionSpec as P

F32 = jnp.float32
BF16 = jnp.bfloat16
AXES = ("curve", "group")
PSEUDO_STEP = 0.05
FACE_SCALE = 0.15


def node_tables():
    points = np.array([-1.0, -1.0 / np.sqrt(5.0), 1.0 / np.sqrt(5.0), 1.0])
    weights = np.array([1.0, 5.0, 5.0, 1.0]) / 6.0
    barycentric = np.array(
        [1.0 / np.prod([points[j] - points[k] for k in range(4) if k != j]) for j in range(4)]
    )
    derivative = np.zeros((4, 4))
    for a in range(4):
        for b in range(4):
            if a != b:
                derivative[a, b] = barycentric[b] / barycentric[a] / (points[a] - points[b])
        derivative[a, a] = -np.sum(derivative[a])
    halves = []
    for upper_half in range(2):
        matrix = np.zeros((4, 4))
        for a in range(4):
            target = 0.5 * points[a] + upper_half - 0.5
            for b in range(4):
                matrix[a, b] = np.prod(
                    [(target - points[k]) / (points[b] - points[k]) for k in range(4) if k != b]
                )
        halves.append(matrix)
    surface_weights = np.kron(weights, weights)
    interpolate = np.stack([np.kron(halves[c // 2], halves[c % 2]) for c in range(4)])
    project = np.stack(
        [
            0.25 * (interpolate[c].T * surface_weights[None, :]) / surface_weights[:, None]
            for c in range(4)
        ]
    )
    return derivative, interpolate, project


def pieces_of(matrix):
    hi = matrix.astype(ml_dtypes.bfloat16)
    lo = (matrix - hi.astype(np.float64)).astype(ml_dtypes.bfloat16)
    return np.concatenate([hi, hi, lo], axis=1)


def operator_tables():
    derivative, interpolate, project = node_tables()
    eye = np.eye(4)
    d_x = np.kron(eye, np.kron(eye, derivative))
    d_y = np.kron(eye, np.kron(derivative, eye))
    d_z = np.kron(derivative, np.kron(eye, eye))
    laplacian = d_x @ d_x + d_y @ d_y + d_z @ d_z
    volume = pieces_of(np.concatenate([d_x, d_y, d_z, laplacian], axis=0))
    return (
        volume,
        pieces_of(interpolate.reshape(64, 16)),
        pieces_of(project.reshape(64, 16)),
    )


def split(x):
    hi = x.astype(BF16)
    lo = (x - hi.astype(F32)).astype(BF16)
    return hi, lo


def dot(a, b):
    return lax.dot_general(a, b, (((1,), (0,)), ((), ())), preferred_element_type=F32)


def one_hot(index, rows):
    place = lax.broadcasted_iota(jnp.int32, (rows, index.shape[1]), 0)
    return jnp.where(place == index, 1.0, 0.0).astype(BF16)


def slot_one_hots(send_ref, recv_ref):
    fine = jnp.where(send_ref[2:3, :] > 0, send_ref[1:2, :] * 128 + send_ref[0:1, :], -1)
    coarse = jnp.where(recv_ref[3:4, :] > 0, recv_ref[1:2, :] * 128 + recv_ref[0:1, :], -1)
    return jnp.concatenate([one_hot(fine, 768), one_hot(coarse, 768)], axis=1)


def by_child(table_ref, values, recv_ref):
    count = len(values)
    hi, lo = split(jnp.concatenate(values, axis=1))
    product = dot(table_ref[...], jnp.concatenate([hi, lo, hi], axis=0))
    child = recv_ref[2:3, :]
    picks = [jnp.where(child == c, 1.0, 0.0) for c in range(4)]
    return [
        sum(
            product[16 * c : 16 * c + 16, 128 * n : 128 * n + 128] * picks[c]
            for c in range(4)
        )
        for n in range(count)
    ]


def face_values(v_ref, face, a):
    d, s = face // 2, face % 2
    if d == 0:
        return v_ref[a, pl.ds(3 * s, 16, stride=4), :]
    if d == 1:
        return jnp.concatenate(
            [v_ref[a, 16 * k + 12 * s : 16 * k + 12 * s + 4, :] for k in range(4)], axis=0
        )
    return v_ref[a, 48 * s : 48 * s + 16, :]


def add_to_face(o_ref, face, a, values):
    d, s = face // 2, face % 2
    if d == 0:
        o_ref[a, pl.ds(3 * s, 16, stride=4), :] += values
    elif d == 1:
        for k in range(4):
            row = 16 * k + 12 * s
            o_ref[a, row : row + 4, :] += values[4 * k : 4 * k + 4]
    else:
        o_ref[a, 48 * s : 48 * s + 16, :] += values


def rims(g_ref):
    odd = jnp.concatenate([g_ref[1], g_ref[3], g_ref[5]], axis=0)
    even = jnp.concatenate([g_ref[0], g_ref[2], g_ref[4]], axis=0)
    lane = lax.broadcasted_iota(jnp.int32, (120, 128), 1)
    up = jnp.where(lane < 64, pltpu.roll(odd[:120], 64, 1), odd[120:])
    down = jnp.where(lane < 64, even[:120], pltpu.roll(even[120:], 64, 1))
    return up, down


def trace_part(v_ref, j_ref, g_ref, h_ref):
    for f in range(6):
        d = f // 2
        w = [face_values(v_ref, f, b) for b in range(5)]
        for a in range(5):
            q = j_ref[a, 0, d : d + 1, :] * w[0]
            for b in range(1, 5):
                q = q + j_ref[a, b, d : d + 1, :] * w[b]
            rows = slice(16 * a, 16 * a + 16)
            plus, minus = (g_ref, h_ref) if f % 2 else (h_ref, g_ref)
            plus[f, rows, :] = w[a] + q
            minus[f, rows, :] = w[a] - q


def pick_slots(t_ref, hots):
    hi, lo = split(jnp.concatenate([t_ref[f] for f in range(6)], axis=1))
    picked = dot(jnp.concatenate([hi, lo], axis=0), hots)
    return picked[:80], picked[80:]


def inter_slots(values, it_ref, recv_ref):
    rows = [values[16 * a : 16 * a + 16] for a in range(5)]
    return jnp.concatenate(by_child(it_ref, rows, recv_ref), axis=0)


def send_part(g_ref, hots, recv_ref, it_ref, edge_ref, m_ref):
    me = lax.axis_index("group")
    up, down = rims(g_ref)
    edge_ref[...] = jnp.where(me == 0, down, up)
    hi, lo = pick_slots(g_ref, hots)
    picked = hi + lo
    outgoing = jnp.concatenate(
        [picked[:, :128], inter_slots(picked[:, 128:], it_ref, recv_ref)], axis=0
    )
    quarter = lax.broadcasted_iota(jnp.int32, (40, 128), 1) // 32
    for t in range(4):
        block = None
        for q in range(4):
            part = outgoing[40 * q : 40 * q + 40]
            shift = (32 * (q - t)) % 128
            part = pltpu.roll(part, shift, 1) if shift else part
            block = part if block is None else jnp.where(quarter == q, part, block)
        m_ref[t, 0:40, :] = block
        m_ref[t, 40:160, :] = jnp.where(me < t, up, down)


def places(nb_ref, f):
    first_id = (lax.axis_index("curve") * 4 + lax.axis_index("group")) * 128
    linked = nb_ref[f : f + 1, :]
    return linked >= 0, linked - first_id


def rim_one_hots(nb_ref, hot_ref):
    for f in range(6):
        linked, place = places(nb_ref, f)
        place = place - 128 if f % 2 else place + 64
        rim = linked & (place >= 0 if f % 2 else place < 64)
        hot = one_hot(jnp.where(rim, place, -1), 64)
        hot_ref[f] = jnp.concatenate([hot, hot], axis=0)


def combine_part(base_ref, loc_ref, edge_ref, m_ref, hot_ref, slot_ref, recv_ref, pt_ref, o_ref):
    me = lax.axis_index("group")
    quarter = lax.broadcasted_iota(jnp.int32, (40, 128), 1) // 32
    parts = []
    for q in range(4):
        part = None
        for s in range(4):
            shift = (32 * (s - q)) % 128
            block = m_ref[s, 0:40, :]
            block = pltpu.roll(block, shift, 1) if shift else block
            part = block if part is None else jnp.where(quarter == s, block, part)
        parts.append(part)
    incoming = jnp.concatenate(parts, axis=0) - loc_ref[...]
    projected = by_child(pt_ref, [incoming[16 * a : 16 * a + 16] for a in range(5)], recv_ref)
    values = jnp.concatenate([incoming[80:160], jnp.concatenate(projected, axis=0)], axis=1)
    hi, lo = split(values)
    spread = lax.dot_general(
        jnp.concatenate([hi, lo], axis=0),
        slot_ref[...],
        (((1,), (1,)), ((), ())),
        preferred_element_type=F32,
    )
    edge = edge_ref[...]
    before = jnp.where(me == 0, edge, m_ref[jnp.maximum(me - 1, 0), 40:160, :])
    after = jnp.where(me == 3, edge, m_ref[jnp.minimum(me + 1, 3), 40:160, :])
    lane = lax.broadcasted_iota(jnp.int32, (120, 128), 1)
    halos = []
    for packed in (before, after):
        hi = packed.astype(BF16).astype(F32)
        lo = packed - hi
        halos.append(
            jnp.concatenate(
                [
                    jnp.where(lane < 64, hi, pltpu.roll(lo, 64, 1)),
                    jnp.where(lane < 64, pltpu.roll(hi, 64, 1), lo),
                ],
                axis=0,
            ).astype(BF16)
        )
    o_ref[...] = base_ref[...]
    for f in range(6):
        third = f // 2
        far = dot(halos[f % 2][80 * third : 80 * third + 80], hot_ref[f])
        columns = slice(128 * f, 128 * f + 128)
        total = (far + spread[:80, columns] + spread[80:, columns]) * (-FACE_SCALE)
        for a in range(5):
            add_to_face(o_ref, f, a, total[16 * a : 16 * a + 16])


def local_part(
    v_ref, j_ref, visc_ref, nb_ref, g_ref, h_ref, slot_ref, recv_ref, vt_ref, it_ref, o_ref, loc_ref
):
    v = v_ref[...]
    hi, lo = split(jnp.concatenate([v[a] for a in range(5)], axis=1))
    terms = dot(vt_ref[...], jnp.concatenate([hi, lo, hi], axis=0))
    visc = visc_ref[...].reshape(1, 128)
    for a in range(5):
        total = visc * terms[192:256, 128 * a : 128 * a + 128]
        for d in range(3):
            for b in range(5):
                total = total - j_ref[a, b, d : d + 1, :] * terms[
                    64 * d : 64 * d + 64, 128 * b : 128 * b + 128
                ]
        o_ref[a] = v[a] - PSEUDO_STEP * total
    for f in range(6):
        linked, place = places(nb_ref, f)
        own = linked & (place < 128 if f % 2 else place >= 0)
        hi, lo = split(g_ref[f ^ 1])
        near = dot(jnp.concatenate([hi, lo], axis=0), one_hot(jnp.where(own, place, -1), 128))
        mask = jnp.where(nb_ref[f : f + 1, :] != -2, FACE_SCALE, 0.0)
        total = mask * h_ref[f] - FACE_SCALE * (near[:80] + near[80:])
        for a in range(5):
            add_to_face(o_ref, f, a, total[16 * a : 16 * a + 16])
    hi, lo = pick_slots(h_ref, slot_ref[...])
    picked = hi + lo
    loc_ref[...] = jnp.concatenate(
        [inter_slots(picked[:, 128:], it_ref, recv_ref), picked[:, :128]], axis=0
    )


def first_kernel(
    v_hbm, j_hbm, send_hbm, recv_hbm, it_hbm,
    g_ref, h_ref, edge_ref, m_ref, slot_ref,
    v_ref, j_ref, send_ref, recv_ref, it_ref, sems,
):
    pairs = (
        (v_hbm, v_ref), (j_hbm, j_ref), (send_hbm, send_ref), (recv_hbm, recv_ref), (it_hbm, it_ref)
    )
    copies = [pltpu.make_async_copy(a, b, sems.at[i]) for i, (a, b) in enumerate(pairs)]
    for copy in copies:
        copy.start()
    for copy in copies:
        copy.wait()
    trace_part(v_ref, j_ref, g_ref, h_ref)
    hots = slot_one_hots(send_ref, recv_ref)
    slot_ref[...] = hots
    send_part(g_ref, hots, recv_ref, it_ref, edge_ref, m_ref)


def first_local(
    v_ref, j_ref, visc_ref, nb_ref, g_ref, h_ref, slot_ref, recv_ref, vt_ref, it_ref,
    o_ref, loc_ref, hot_ref,
):
    rim_one_hots(nb_ref, hot_ref)
    local_part(
        v_ref, j_ref, visc_ref, nb_ref, g_ref, h_ref, slot_ref, recv_ref, vt_ref, it_ref, o_ref, loc_ref
    )


def middle_kernel(
    base_ref, loc_ref, edge_ref, m_ref, hot_ref, slot_ref, recv_ref, pt_ref, j_ref, it_ref,
    o_ref, g_ref, h_ref, edge2_ref, m2_ref,
):
    combine_part(base_ref, loc_ref, edge_ref, m_ref, hot_ref, slot_ref, recv_ref, pt_ref, o_ref)
    trace_part(o_ref, j_ref, g_ref, h_ref)
    send_part(g_ref, slot_ref[...], recv_ref, it_ref, edge2_ref, m2_ref)


def shape(*dims, kind=F32):
    return jax.ShapeDtypeStruct(dims, kind)


PARAMS = pltpu.CompilerParams(vmem_limit_bytes=32 * 1024 * 1024)


def call(kernel, outs, *args):
    return pl.pallas_call(kernel, out_shape=outs, compiler_params=PARAMS)(*args)


def call_from_hbm(kernel, outs, *args):
    args = [pltpu.with_memory_space_constraint(x, pltpu.HBM) for x in args]
    return pl.pallas_call(
        kernel,
        out_shape=outs,
        in_specs=[pl.BlockSpec(memory_space=pltpu.HBM)] * len(args),
        scratch_shapes=[pltpu.VMEM(x.shape, x.dtype) for x in args]
        + [pltpu.SemaphoreType.DMA((len(args),))],
        compiler_params=PARAMS,
    )(*args)


IMAGE = shape(5, 64, 128)
TRACES = shape(6, 80, 128)
EDGE = shape(120, 128)
SLOTS = shape(160, 128)
MESSAGE = shape(4, 160, 128)
SLOT_HOTS = shape(768, 256, kind=BF16)
RIM_HOTS = shape(6, 128, 128, kind=BF16)


def exchange(edge, message):
    ends = [(4 * c + 3, 4 * c + 4) for c in range(lax.axis_size("curve") - 1)]
    message = lax.all_to_all(message, "group", split_axis=0, concat_axis=0, tiled=True)
    edge = lax.ppermute(edge, AXES, ends + [(j, i) for i, j in ends])
    return edge, message


def local(tangent, jacobian, viscosity, neighbours, send_table, recv_table):
    volume_table, inter_table, project_table = (jnp.asarray(t) for t in operator_tables())
    jacobian = jnp.transpose(jacobian, (1, 2, 0, 3))
    g, h, edge, message, slots = call_from_hbm(
        first_kernel,
        (TRACES, TRACES, EDGE, MESSAGE, SLOT_HOTS),
        tangent, jacobian, send_table, recv_table, inter_table,
    )
    edge, message = exchange(edge, message)
    base, loc, hots = call(
        first_local,
        (IMAGE, SLOTS, RIM_HOTS),
        tangent, jacobian, viscosity, neighbours, g, h, slots, recv_table, volume_table, inter_table,
    )
    first, g, h, edge, message = call(
        middle_kernel,
        (IMAGE, TRACES, TRACES, EDGE, MESSAGE),
        base, loc, edge, message, hots, slots, recv_table, project_table, jacobian, inter_table,
    )
    edge, message = exchange(edge, message)
    base, loc = call(
        local_part,
        (IMAGE, SLOTS),
        first, jacobian, viscosity, neighbours, g, h, slots, recv_table, volume_table, inter_table,
    )
    second = call(
        combine_part, IMAGE, base, loc, edge, message, hots, slots, recv_table, project_table
    )
    return first, second


def solution(mesh):
    in_specs = (
        P(None, None, AXES),
        P(None, None, None, AXES),
        P(AXES),
        P(None, AXES),
        P(None, AXES),
        P(None, AXES),
    )
    out_specs = (P(None, None, AXES), P(None, None, AXES))
    return jax.shard_map(local, mesh=mesh, in_specs=in_specs, out_specs=out_specs, check_vma=False)
```

```python
import jax
import jax.numpy as jnp
import ml_dtypes
import numpy as np
from jax import lax
from jax.experimental import pallas as pl
from jax.experimental.pallas import tpu as pltpu
from jax.sharding import PartitionSpec as P

F32 = jnp.float32
BF16 = jnp.bfloat16
AXES = ("curve", "group")
PSEUDO_STEP = 0.05
FACE_SCALE = 0.15


def node_tables():
    points = np.array([-1.0, -1.0 / np.sqrt(5.0), 1.0 / np.sqrt(5.0), 1.0])
    weights = np.array([1.0, 5.0, 5.0, 1.0]) / 6.0
    barycentric = np.array(
        [1.0 / np.prod([points[j] - points[k] for k in range(4) if k != j]) for j in range(4)]
    )
    derivative = np.zeros((4, 4))
    for a in range(4):
        for b in range(4):
            if a != b:
                derivative[a, b] = barycentric[b] / barycentric[a] / (points[a] - points[b])
        derivative[a, a] = -np.sum(derivative[a])
    halves = []
    for upper_half in range(2):
        matrix = np.zeros((4, 4))
        for a in range(4):
            target = 0.5 * points[a] + upper_half - 0.5
            for b in range(4):
                matrix[a, b] = np.prod(
                    [(target - points[k]) / (points[b] - points[k]) for k in range(4) if k != b]
                )
        halves.append(matrix)
    surface_weights = np.kron(weights, weights)
    interpolate = np.stack([np.kron(halves[c // 2], halves[c % 2]) for c in range(4)])
    project = np.stack(
        [
            0.25 * (interpolate[c].T * surface_weights[None, :]) / surface_weights[:, None]
            for c in range(4)
        ]
    )
    return derivative, interpolate, project


def pieces_of(matrix):
    hi = matrix.astype(ml_dtypes.bfloat16)
    lo = (matrix - hi.astype(np.float64)).astype(ml_dtypes.bfloat16)
    return np.concatenate([hi, hi, lo], axis=1)


def operator_tables():
    derivative, interpolate, project = node_tables()
    eye = np.eye(4)
    d_x = np.kron(eye, np.kron(eye, derivative))
    d_y = np.kron(eye, np.kron(derivative, eye))
    d_z = np.kron(derivative, np.kron(eye, eye))
    laplacian = d_x @ d_x + d_y @ d_y + d_z @ d_z
    volume = pieces_of(np.concatenate([d_x, d_y, d_z, laplacian], axis=0))
    return (
        volume,
        pieces_of(interpolate.reshape(64, 16)),
        pieces_of(project.reshape(64, 16)),
    )


def split(x):
    hi = x.astype(BF16)
    lo = (x - hi.astype(F32)).astype(BF16)
    return hi, lo


def dot(a, b):
    return lax.dot_general(a, b, (((1,), (0,)), ((), ())), preferred_element_type=F32)


def one_hot(index, rows):
    place = lax.broadcasted_iota(jnp.int32, (rows, index.shape[1]), 0)
    return jnp.where(place == index, 1.0, 0.0).astype(BF16)


def slot_one_hots(send_ref, recv_ref):
    fine = jnp.where(send_ref[2:3, :] > 0, send_ref[1:2, :] * 128 + send_ref[0:1, :], -1)
    coarse = jnp.where(recv_ref[3:4, :] > 0, recv_ref[1:2, :] * 128 + recv_ref[0:1, :], -1)
    return jnp.concatenate([one_hot(fine, 768), one_hot(coarse, 768)], axis=1)


def by_child(table_ref, values, recv_ref):
    count = len(values)
    hi, lo = split(jnp.concatenate(values, axis=1))
    product = dot(table_ref[...], jnp.concatenate([hi, lo, hi], axis=0))
    child = recv_ref[2:3, :]
    picks = [jnp.where(child == c, 1.0, 0.0) for c in range(4)]
    return [
        sum(
            product[16 * c : 16 * c + 16, 128 * n : 128 * n + 128] * picks[c]
            for c in range(4)
        )
        for n in range(count)
    ]


def face_values(v_ref, face, a):
    d, s = face // 2, face % 2
    if d == 0:
        return v_ref[a, pl.ds(3 * s, 16, stride=4), :]
    if d == 1:
        return jnp.concatenate(
            [v_ref[a, 16 * k + 12 * s : 16 * k + 12 * s + 4, :] for k in range(4)], axis=0
        )
    return v_ref[a, 48 * s : 48 * s + 16, :]


def add_to_face(o_ref, face, a, values):
    d, s = face // 2, face % 2
    if d == 0:
        o_ref[a, pl.ds(3 * s, 16, stride=4), :] += values
    elif d == 1:
        for k in range(4):
            row = 16 * k + 12 * s
            o_ref[a, row : row + 4, :] += values[4 * k : 4 * k + 4]
    else:
        o_ref[a, 48 * s : 48 * s + 16, :] += values


def rims(g_ref):
    odd = jnp.concatenate([g_ref[1], g_ref[3], g_ref[5]], axis=0)
    even = jnp.concatenate([g_ref[0], g_ref[2], g_ref[4]], axis=0)
    lane = lax.broadcasted_iota(jnp.int32, (120, 128), 1)
    up = jnp.where(lane < 64, pltpu.roll(odd[:120], 64, 1), odd[120:])
    down = jnp.where(lane < 64, even[:120], pltpu.roll(even[120:], 64, 1))
    return up, down


def trace_part(v_ref, j_ref, g_ref, h_ref):
    for f in range(6):
        d = f // 2
        w = [face_values(v_ref, f, b) for b in range(5)]
        for a in range(5):
            q = j_ref[a, 0, d : d + 1, :] * w[0]
            for b in range(1, 5):
                q = q + j_ref[a, b, d : d + 1, :] * w[b]
            rows = slice(16 * a, 16 * a + 16)
            plus, minus = (g_ref, h_ref) if f % 2 else (h_ref, g_ref)
            plus[f, rows, :] = w[a] + q
            minus[f, rows, :] = w[a] - q


def pick_slots(t_ref, hots):
    hi, lo = split(jnp.concatenate([t_ref[f] for f in range(6)], axis=1))
    picked = dot(jnp.concatenate([hi, lo], axis=0), hots)
    return picked[:80], picked[80:]


def inter_slots(values, it_ref, recv_ref):
    rows = [values[16 * a : 16 * a + 16] for a in range(5)]
    return jnp.concatenate(by_child(it_ref, rows, recv_ref), axis=0)


def send_part(g_ref, hots, recv_ref, it_ref, edge_ref, m_ref, m_hbm, sems):
    me = lax.axis_index("group")
    up, down = rims(g_ref)
    edge_ref[...] = jnp.where(me == 0, down, up)
    for t in range(4):
        m_ref[t, 40:160, :] = jnp.where(me < t, up, down)
    rim_copy = pltpu.make_async_copy(
        m_ref.at[:, pl.ds(40, 120), :], m_hbm.at[:, pl.ds(40, 120), :], sems.at[0]
    )
    rim_copy.start()
    hi, lo = pick_slots(g_ref, hots)
    picked = hi + lo
    outgoing = jnp.concatenate(
        [picked[:, :128], inter_slots(picked[:, 128:], it_ref, recv_ref)], axis=0
    )
    quarter = lax.broadcasted_iota(jnp.int32, (40, 128), 1) // 32
    for t in range(4):
        block = None
        for q in range(4):
            part = outgoing[40 * q : 40 * q + 40]
            shift = (32 * (q - t)) % 128
            part = pltpu.roll(part, shift, 1) if shift else part
            block = part if block is None else jnp.where(quarter == q, part, block)
        m_ref[t, 0:40, :] = block
    slot_copy = pltpu.make_async_copy(
        m_ref.at[:, pl.ds(0, 40), :], m_hbm.at[:, pl.ds(0, 40), :], sems.at[1]
    )
    slot_copy.start()
    rim_copy.wait()
    slot_copy.wait()


def places(nb_ref, f):
    first_id = (lax.axis_index("curve") * 4 + lax.axis_index("group")) * 128
    linked = nb_ref[f : f + 1, :]
    return linked >= 0, linked - first_id


def rim_one_hots(nb_ref, hot_ref):
    for f in range(6):
        linked, place = places(nb_ref, f)
        place = place - 128 if f % 2 else place + 64
        rim = linked & (place >= 0 if f % 2 else place < 64)
        hot = one_hot(jnp.where(rim, place, -1), 64)
        hot_ref[f] = jnp.concatenate([hot, hot], axis=0)


def rim_pieces(packed):
    lane = lax.broadcasted_iota(jnp.int32, (120, 128), 1)
    hi = packed.astype(BF16).astype(F32)
    lo = packed - hi
    return jnp.concatenate(
        [
            jnp.where(lane < 64, hi, pltpu.roll(lo, 64, 1)),
            jnp.where(lane < 64, pltpu.roll(hi, 64, 1), lo),
        ],
        axis=0,
    ).astype(BF16)


def group_part(base_ref, loc_ref, m_ref, hot_ref, slot_ref, recv_ref, pt_ref, o_ref):
    me = lax.axis_index("group")
    quarter = lax.broadcasted_iota(jnp.int32, (40, 128), 1) // 32
    parts = []
    for q in range(4):
        part = None
        for s in range(4):
            shift = (32 * (s - q)) % 128
            block = m_ref[s, 0:40, :]
            block = pltpu.roll(block, shift, 1) if shift else block
            part = block if part is None else jnp.where(quarter == s, block, part)
        parts.append(part)
    incoming = jnp.concatenate(parts, axis=0) - loc_ref[...]
    projected = by_child(pt_ref, [incoming[16 * a : 16 * a + 16] for a in range(5)], recv_ref)
    values = jnp.concatenate([incoming[80:160], jnp.concatenate(projected, axis=0)], axis=1)
    hi, lo = split(values)
    spread = lax.dot_general(
        jnp.concatenate([hi, lo], axis=0),
        slot_ref[...],
        (((1,), (1,)), ((), ())),
        preferred_element_type=F32,
    )
    before = jnp.where(me == 0, 0.0, m_ref[jnp.maximum(me - 1, 0), 40:160, :])
    after = jnp.where(me == 3, 0.0, m_ref[jnp.minimum(me + 1, 3), 40:160, :])
    halos = [rim_pieces(before), rim_pieces(after)]
    o_ref[...] = base_ref[...]
    for f in range(6):
        third = f // 2
        far = dot(halos[f % 2][80 * third : 80 * third + 80], hot_ref[f])
        columns = slice(128 * f, 128 * f + 128)
        total = (far + spread[:80, columns] + spread[80:, columns]) * (-FACE_SCALE)
        for a in range(5):
            add_to_face(o_ref, f, a, total[16 * a : 16 * a + 16])


def edge_part(base_ref, edge_ref, hot_ref, o_ref):
    me = lax.axis_index("group")
    o_ref[...] = base_ref[...]
    for end, parity in ((0, 0), (3, 1)):

        @pl.when(me == end)
        def _():
            halo = rim_pieces(edge_ref[...])
            for third in range(3):
                f = 2 * third + parity
                far = dot(halo[80 * third : 80 * third + 80], hot_ref[f]) * (-FACE_SCALE)
                for a in range(5):
                    add_to_face(o_ref, f, a, far[16 * a : 16 * a + 16])


def local_part(
    v_ref, j_ref, visc_ref, nb_ref, g_ref, h_ref, slot_ref, recv_ref, vt_ref, it_ref, o_ref, loc_ref
):
    v = v_ref[...]
    hi, lo = split(jnp.concatenate([v[a] for a in range(5)], axis=1))
    terms = dot(vt_ref[...], jnp.concatenate([hi, lo, hi], axis=0))
    visc = visc_ref[...].reshape(1, 128)
    for a in range(5):
        total = visc * terms[192:256, 128 * a : 128 * a + 128]
        for d in range(3):
            for b in range(5):
                total = total - j_ref[a, b, d : d + 1, :] * terms[
                    64 * d : 64 * d + 64, 128 * b : 128 * b + 128
                ]
        o_ref[a] = v[a] - PSEUDO_STEP * total
    for f in range(6):
        linked, place = places(nb_ref, f)
        own = linked & (place < 128 if f % 2 else place >= 0)
        hi, lo = split(g_ref[f ^ 1])
        near = dot(jnp.concatenate([hi, lo], axis=0), one_hot(jnp.where(own, place, -1), 128))
        mask = jnp.where(nb_ref[f : f + 1, :] != -2, FACE_SCALE, 0.0)
        total = mask * h_ref[f] - FACE_SCALE * (near[:80] + near[80:])
        for a in range(5):
            add_to_face(o_ref, f, a, total[16 * a : 16 * a + 16])
    hi, lo = pick_slots(h_ref, slot_ref[...])
    picked = hi + lo
    loc_ref[...] = jnp.concatenate(
        [inter_slots(picked[:, 128:], it_ref, recv_ref), picked[:, :128]], axis=0
    )


def first_kernel(
    v_hbm, j_hbm, send_hbm, recv_hbm, it_hbm,
    g_ref, h_ref, edge_ref, m_hbm, slot_ref,
    v_ref, j_ref, send_ref, recv_ref, it_ref, m_ref, sems, m_sems,
):
    pairs = (
        (v_hbm, v_ref), (j_hbm, j_ref), (send_hbm, send_ref), (recv_hbm, recv_ref), (it_hbm, it_ref)
    )
    copies = [pltpu.make_async_copy(a, b, sems.at[i]) for i, (a, b) in enumerate(pairs)]
    for copy in copies:
        copy.start()
    for copy in copies[2:]:
        copy.wait()
    slot_ref[...] = slot_one_hots(send_ref, recv_ref)
    for copy in copies[:2]:
        copy.wait()
    trace_part(v_ref, j_ref, g_ref, h_ref)
    send_part(g_ref, slot_ref[...], recv_ref, it_ref, edge_ref, m_ref, m_hbm, m_sems)


def first_local(
    v_ref, j_ref, visc_ref, nb_ref, g_ref, h_ref, slot_ref, recv_ref, vt_ref, it_ref,
    o_ref, loc_ref, hot_ref,
):
    rim_one_hots(nb_ref, hot_ref)
    local_part(
        v_ref, j_ref, visc_ref, nb_ref, g_ref, h_ref, slot_ref, recv_ref, vt_ref, it_ref, o_ref, loc_ref
    )


def second_local(
    v_ref, j_ref, visc_ref, nb_ref, g_ref, h_ref, slot_ref, recv_ref, vt_ref, it_ref,
    o_ref, loc_ref, v_hbm, sem,
):
    copy = pltpu.make_async_copy(v_ref, v_hbm, sem)
    copy.start()
    local_part(
        v_ref, j_ref, visc_ref, nb_ref, g_ref, h_ref, slot_ref, recv_ref, vt_ref, it_ref, o_ref, loc_ref
    )
    copy.wait()


def middle_kernel(
    base_ref, edge_ref, hot_ref, slot_ref, recv_ref, j_ref, it_ref,
    o_ref, g_ref, h_ref, edge2_ref, m_hbm,
    m_ref, m_sems,
):
    edge_part(base_ref, edge_ref, hot_ref, o_ref)
    trace_part(o_ref, j_ref, g_ref, h_ref)
    send_part(g_ref, slot_ref[...], recv_ref, it_ref, edge2_ref, m_ref, m_hbm, m_sems)


def shape(*dims, kind=F32):
    return jax.ShapeDtypeStruct(dims, kind)


PARAMS = pltpu.CompilerParams(vmem_limit_bytes=32 * 1024 * 1024)


def call(kernel, outs, *args):
    return pl.pallas_call(kernel, out_shape=outs, compiler_params=PARAMS)(*args)


IMAGE = shape(5, 64, 128)
TRACES = shape(6, 80, 128)
EDGE = shape(120, 128)
SLOTS = shape(160, 128)
MESSAGE = shape(4, 160, 128)
SLOT_HOTS = shape(768, 256, kind=BF16)
RIM_HOTS = shape(6, 128, 128, kind=BF16)


def exchange(edge, message):
    ends = [(4 * c + 3, 4 * c + 4) for c in range(lax.axis_size("curve") - 1)]
    message = lax.all_to_all(message, "group", split_axis=0, concat_axis=0, tiled=True)
    edge = lax.ppermute(edge, AXES, ends + [(j, i) for i, j in ends])
    return edge, message


VMEM = pl.BlockSpec(memory_space=pltpu.VMEM)
HBM = pl.BlockSpec(memory_space=pltpu.HBM)
MESSAGE_SCRATCH = [pltpu.VMEM(MESSAGE.shape, F32)]
TWO_COPIES = pltpu.SemaphoreType.DMA((2,))


def local(tangent, jacobian, viscosity, neighbours, send_table, recv_table):
    volume_table, inter_table, project_table = (jnp.asarray(t) for t in operator_tables())
    jacobian = jnp.transpose(jacobian, (1, 2, 0, 3))
    inputs = (tangent, jacobian, send_table, recv_table, inter_table)
    g, h, edge, message, slots = pl.pallas_call(
        first_kernel,
        out_shape=(TRACES, TRACES, EDGE, MESSAGE, SLOT_HOTS),
        in_specs=[HBM] * 5,
        out_specs=(VMEM, VMEM, VMEM, HBM, VMEM),
        scratch_shapes=[pltpu.VMEM(x.shape, x.dtype) for x in inputs]
        + MESSAGE_SCRATCH
        + [pltpu.SemaphoreType.DMA((5,)), TWO_COPIES],
        compiler_params=PARAMS,
    )(*(pltpu.with_memory_space_constraint(x, pltpu.HBM) for x in inputs))
    edge, message = exchange(edge, message)
    base, loc, hots = call(
        first_local,
        (IMAGE, SLOTS, RIM_HOTS),
        tangent, jacobian, viscosity, neighbours, g, h, slots, recv_table, volume_table, inter_table,
    )
    base = call(group_part, IMAGE, base, loc, message, hots, slots, recv_table, project_table)
    image, g, h, edge, message = pl.pallas_call(
        middle_kernel,
        out_shape=(pltpu.VMEM(IMAGE.shape, F32), TRACES, TRACES, EDGE, MESSAGE),
        in_specs=[VMEM] * 7,
        out_specs=(VMEM, VMEM, VMEM, VMEM, HBM),
        scratch_shapes=MESSAGE_SCRATCH + [TWO_COPIES],
        compiler_params=PARAMS,
    )(base, edge, hots, slots, recv_table, jacobian, inter_table)
    edge, message = exchange(edge, message)
    base, loc, first = pl.pallas_call(
        second_local,
        out_shape=(IMAGE, SLOTS, IMAGE),
        in_specs=[VMEM] * 10,
        out_specs=(VMEM, VMEM, HBM),
        scratch_shapes=[pltpu.SemaphoreType.DMA],
        compiler_params=PARAMS,
    )(image, jacobian, viscosity, neighbours, g, h, slots, recv_table, volume_table, inter_table)
    base = call(group_part, IMAGE, base, loc, message, hots, slots, recv_table, project_table)
    second = call(edge_part, IMAGE, base, edge, hots)
    return first, second


def solution(mesh):
    in_specs = (
        P(None, None, AXES),
        P(None, None, None, AXES),
        P(AXES),
        P(None, AXES),
        P(None, AXES),
        P(None, AXES),
    )
    out_specs = (P(None, None, AXES), P(None, None, AXES))
    return jax.shard_map(local, mesh=mesh, in_specs=in_specs, out_specs=out_specs, check_vma=False)
```

```python
import jax
import jax.numpy as jnp
import ml_dtypes
import numpy as np
from jax import lax
from jax.experimental import pallas as pl
from jax.experimental.pallas import tpu as pltpu
from jax.sharding import PartitionSpec as P

F32 = jnp.float32
BF16 = jnp.bfloat16
AXES = ("curve", "group")
PSEUDO_STEP = 0.05
FACE_SCALE = 0.15


def node_tables():
    points = np.array([-1.0, -1.0 / np.sqrt(5.0), 1.0 / np.sqrt(5.0), 1.0])
    weights = np.array([1.0, 5.0, 5.0, 1.0]) / 6.0
    barycentric = np.array(
        [1.0 / np.prod([points[j] - points[k] for k in range(4) if k != j]) for j in range(4)]
    )
    derivative = np.zeros((4, 4))
    for a in range(4):
        for b in range(4):
            if a != b:
                derivative[a, b] = barycentric[b] / barycentric[a] / (points[a] - points[b])
        derivative[a, a] = -np.sum(derivative[a])
    halves = []
    for upper_half in range(2):
        matrix = np.zeros((4, 4))
        for a in range(4):
            target = 0.5 * points[a] + upper_half - 0.5
            for b in range(4):
                matrix[a, b] = np.prod(
                    [(target - points[k]) / (points[b] - points[k]) for k in range(4) if k != b]
                )
        halves.append(matrix)
    surface_weights = np.kron(weights, weights)
    interpolate = np.stack([np.kron(halves[c // 2], halves[c % 2]) for c in range(4)])
    project = np.stack(
        [
            0.25 * (interpolate[c].T * surface_weights[None, :]) / surface_weights[:, None]
            for c in range(4)
        ]
    )
    return derivative, interpolate, project


def pieces_of(matrix):
    hi = matrix.astype(ml_dtypes.bfloat16)
    lo = (matrix - hi.astype(np.float64)).astype(ml_dtypes.bfloat16)
    return np.concatenate([hi, hi, lo], axis=1)


def operator_tables():
    derivative, interpolate, project = node_tables()
    eye = np.eye(4)
    d_x = np.kron(eye, np.kron(eye, derivative))
    d_y = np.kron(eye, np.kron(derivative, eye))
    d_z = np.kron(derivative, np.kron(eye, eye))
    laplacian = d_x @ d_x + d_y @ d_y + d_z @ d_z
    volume = pieces_of(np.concatenate([d_x, d_y, d_z, laplacian], axis=0))
    return (
        volume,
        pieces_of(interpolate.reshape(64, 16)),
        pieces_of(project.reshape(64, 16)),
    )


def split(x):
    hi = x.astype(BF16)
    lo = (x - hi.astype(F32)).astype(BF16)
    return hi, lo


def dot(a, b):
    return lax.dot_general(a, b, (((1,), (0,)), ((), ())), preferred_element_type=F32)


def one_hot(index, rows):
    place = lax.broadcasted_iota(jnp.int32, (rows, index.shape[1]), 0)
    return jnp.where(place == index, 1.0, 0.0).astype(BF16)


def slot_one_hots(send_ref, recv_ref):
    fine = jnp.where(send_ref[2:3, :] > 0, send_ref[1:2, :] * 128 + send_ref[0:1, :], -1)
    coarse = jnp.where(recv_ref[3:4, :] > 0, recv_ref[1:2, :] * 128 + recv_ref[0:1, :], -1)
    return jnp.concatenate([one_hot(fine, 768), one_hot(coarse, 768)], axis=1)


def by_child(table_ref, values, recv_ref):
    count = len(values)
    hi, lo = split(jnp.concatenate(values, axis=1))
    product = dot(table_ref[...], jnp.concatenate([hi, lo, hi], axis=0))
    child = recv_ref[2:3, :]
    picks = [jnp.where(child == c, 1.0, 0.0) for c in range(4)]
    return [
        sum(
            product[16 * c : 16 * c + 16, 128 * n : 128 * n + 128] * picks[c]
            for c in range(4)
        )
        for n in range(count)
    ]


def face_values(v_ref, face, a):
    d, s = face // 2, face % 2
    if d == 0:
        return v_ref[a, pl.ds(3 * s, 16, stride=4), :]
    if d == 1:
        return jnp.concatenate(
            [v_ref[a, 16 * k + 12 * s : 16 * k + 12 * s + 4, :] for k in range(4)], axis=0
        )
    return v_ref[a, 48 * s : 48 * s + 16, :]


def add_to_face(o_ref, face, a, values):
    d, s = face // 2, face % 2
    if d == 0:
        o_ref[a, pl.ds(3 * s, 16, stride=4), :] += values
    elif d == 1:
        for k in range(4):
            row = 16 * k + 12 * s
            o_ref[a, row : row + 4, :] += values[4 * k : 4 * k + 4]
    else:
        o_ref[a, 48 * s : 48 * s + 16, :] += values


def rims(g_ref):
    odd = jnp.concatenate([g_ref[1], g_ref[3], g_ref[5]], axis=0)
    even = jnp.concatenate([g_ref[0], g_ref[2], g_ref[4]], axis=0)
    lane = lax.broadcasted_iota(jnp.int32, (120, 128), 1)
    up = jnp.where(lane < 64, pltpu.roll(odd[:120], 64, 1), odd[120:])
    down = jnp.where(lane < 64, even[:120], pltpu.roll(even[120:], 64, 1))
    return up, down


def trace_part(v_ref, j_ref, g_ref, h_ref):
    for f in range(6):
        d = f // 2
        w = [face_values(v_ref, f, b) for b in range(5)]
        for a in range(5):
            q = j_ref[a, 0, d : d + 1, :] * w[0]
            for b in range(1, 5):
                q = q + j_ref[a, b, d : d + 1, :] * w[b]
            rows = slice(16 * a, 16 * a + 16)
            plus, minus = (g_ref, h_ref) if f % 2 else (h_ref, g_ref)
            plus[f, rows, :] = w[a] + q
            minus[f, rows, :] = w[a] - q


def pick_slots(t_ref, hots):
    hi, lo = split(jnp.concatenate([t_ref[f] for f in range(6)], axis=1))
    picked = dot(jnp.concatenate([hi, lo], axis=0), hots)
    return picked[:80], picked[80:]


def inter_slots(values, it_ref, recv_ref):
    rows = [values[16 * a : 16 * a + 16] for a in range(5)]
    return jnp.concatenate(by_child(it_ref, rows, recv_ref), axis=0)


def send_part(g_ref, hots, recv_ref, it_ref, edge_ref, m_ref, m_hbm, sems):
    me = lax.axis_index("group")
    up, down = rims(g_ref)
    edge_ref[...] = jnp.where(me == 0, down, up)
    for t in range(4):
        m_ref[t, 40:160, :] = jnp.where(me < t, up, down)
    rim_copy = pltpu.make_async_copy(
        m_ref.at[:, pl.ds(40, 120), :], m_hbm.at[:, pl.ds(40, 120), :], sems.at[0]
    )
    rim_copy.start()
    hi, lo = pick_slots(g_ref, hots)
    picked = hi + lo
    outgoing = jnp.concatenate(
        [picked[:, :128], inter_slots(picked[:, 128:], it_ref, recv_ref)], axis=0
    )
    quarter = lax.broadcasted_iota(jnp.int32, (40, 128), 1) // 32
    for t in range(4):
        block = None
        for q in range(4):
            part = outgoing[40 * q : 40 * q + 40]
            shift = (32 * (q - t)) % 128
            part = pltpu.roll(part, shift, 1) if shift else part
            block = part if block is None else jnp.where(quarter == q, part, block)
        m_ref[t, 0:40, :] = block
    slot_copy = pltpu.make_async_copy(
        m_ref.at[:, pl.ds(0, 40), :], m_hbm.at[:, pl.ds(0, 40), :], sems.at[1]
    )
    slot_copy.start()
    rim_copy.wait()
    slot_copy.wait()


def places(nb_ref, f):
    first_id = (lax.axis_index("curve") * 4 + lax.axis_index("group")) * 128
    linked = nb_ref[f : f + 1, :]
    return linked >= 0, linked - first_id


def rim_one_hots(nb_ref, hot_ref):
    for f in range(6):
        linked, place = places(nb_ref, f)
        place = place - 128 if f % 2 else place + 64
        rim = linked & (place >= 0 if f % 2 else place < 64)
        hot = one_hot(jnp.where(rim, place, -1), 64)
        hot_ref[f] = jnp.concatenate([hot, hot], axis=0)


def rim_pieces(packed):
    lane = lax.broadcasted_iota(jnp.int32, (120, 128), 1)
    hi = packed.astype(BF16).astype(F32)
    lo = packed - hi
    return jnp.concatenate(
        [
            jnp.where(lane < 64, hi, pltpu.roll(lo, 64, 1)),
            jnp.where(lane < 64, pltpu.roll(hi, 64, 1), lo),
        ],
        axis=0,
    ).astype(BF16)


def group_part(base_ref, loc_ref, m_ref, hot_ref, slot_ref, recv_ref, pt_ref, o_ref):
    me = lax.axis_index("group")
    quarter = lax.broadcasted_iota(jnp.int32, (40, 128), 1) // 32
    parts = []
    for q in range(4):
        part = None
        for s in range(4):
            shift = (32 * (s - q)) % 128
            block = m_ref[s, 0:40, :]
            block = pltpu.roll(block, shift, 1) if shift else block
            part = block if part is None else jnp.where(quarter == s, block, part)
        parts.append(part)
    incoming = jnp.concatenate(parts, axis=0) - loc_ref[...]
    projected = by_child(pt_ref, [incoming[16 * a : 16 * a + 16] for a in range(5)], recv_ref)
    values = jnp.concatenate([incoming[80:160], jnp.concatenate(projected, axis=0)], axis=1)
    hi, lo = split(values)
    spread = lax.dot_general(
        jnp.concatenate([hi, lo], axis=0),
        slot_ref[...],
        (((1,), (1,)), ((), ())),
        preferred_element_type=F32,
    )
    before = jnp.where(me == 0, 0.0, m_ref[jnp.maximum(me - 1, 0), 40:160, :])
    after = jnp.where(me == 3, 0.0, m_ref[jnp.minimum(me + 1, 3), 40:160, :])
    halos = [rim_pieces(before), rim_pieces(after)]
    o_ref[...] = base_ref[...]
    for f in range(6):
        third = f // 2
        far = dot(halos[f % 2][80 * third : 80 * third + 80], hot_ref[f])
        columns = slice(128 * f, 128 * f + 128)
        total = (far + spread[:80, columns] + spread[80:, columns]) * (-FACE_SCALE)
        for a in range(5):
            add_to_face(o_ref, f, a, total[16 * a : 16 * a + 16])


def edge_part(base_ref, edge_ref, hot_ref, o_ref):
    me = lax.axis_index("group")
    o_ref[...] = base_ref[...]
    for end, parity in ((0, 0), (3, 1)):

        @pl.when(me == end)
        def _():
            halo = rim_pieces(edge_ref[...])
            for third in range(3):
                f = 2 * third + parity
                far = dot(halo[80 * third : 80 * third + 80], hot_ref[f]) * (-FACE_SCALE)
                for a in range(5):
                    add_to_face(o_ref, f, a, far[16 * a : 16 * a + 16])


def slot_terms(h_ref, slot_ref, recv_ref, it_ref, loc_ref):
    hi, lo = pick_slots(h_ref, slot_ref[...])
    picked = hi + lo
    loc_ref[...] = jnp.concatenate(
        [inter_slots(picked[:, 128:], it_ref, recv_ref), picked[:, :128]], axis=0
    )


def local_part(v_ref, j_ref, visc_ref, nb_ref, g_ref, h_ref, vt_ref, o_ref):
    v = v_ref[...]
    hi, lo = split(jnp.concatenate([v[a] for a in range(5)], axis=1))
    terms = dot(vt_ref[...], jnp.concatenate([hi, lo, hi], axis=0))
    visc = visc_ref[...].reshape(1, 128)
    for a in range(5):
        total = visc * terms[192:256, 128 * a : 128 * a + 128]
        for d in range(3):
            for b in range(5):
                total = total - j_ref[a, b, d : d + 1, :] * terms[
                    64 * d : 64 * d + 64, 128 * b : 128 * b + 128
                ]
        o_ref[a] = v[a] - PSEUDO_STEP * total
    for f in range(6):
        linked, place = places(nb_ref, f)
        own = linked & (place < 128 if f % 2 else place >= 0)
        hi, lo = split(g_ref[f ^ 1])
        near = dot(jnp.concatenate([hi, lo], axis=0), one_hot(jnp.where(own, place, -1), 128))
        mask = jnp.where(nb_ref[f : f + 1, :] != -2, FACE_SCALE, 0.0)
        total = mask * h_ref[f] - FACE_SCALE * (near[:80] + near[80:])
        for a in range(5):
            add_to_face(o_ref, f, a, total[16 * a : 16 * a + 16])


def first_kernel(
    v_hbm, j_hbm, send_hbm, recv_hbm, it_hbm,
    g_ref, h_ref, edge_ref, m_hbm, slot_ref, v_ref, j_ref, recv_ref, it_ref,
    send_ref, m_ref, sems, m_sems,
):
    pairs = (
        (v_hbm, v_ref), (j_hbm, j_ref), (send_hbm, send_ref), (recv_hbm, recv_ref), (it_hbm, it_ref)
    )
    copies = [pltpu.make_async_copy(a, b, sems.at[i]) for i, (a, b) in enumerate(pairs)]
    for copy in copies:
        copy.start()
    for copy in copies[2:]:
        copy.wait()
    slot_ref[...] = slot_one_hots(send_ref, recv_ref)
    for copy in copies[:2]:
        copy.wait()
    trace_part(v_ref, j_ref, g_ref, h_ref)
    send_part(g_ref, slot_ref[...], recv_ref, it_ref, edge_ref, m_ref, m_hbm, m_sems)


def first_local(
    v_ref, j_ref, g_ref, h_ref, slot_ref, recv_ref, it_ref, visc_hbm, nb_hbm, vt_hbm, pt_hbm,
    o_ref, loc_ref, hot_ref, visc_ref, nb_ref, vt_ref, pt_ref, sems,
):
    pairs = ((visc_hbm, visc_ref), (nb_hbm, nb_ref), (vt_hbm, vt_ref), (pt_hbm, pt_ref))
    copies = [pltpu.make_async_copy(a, b, sems.at[i]) for i, (a, b) in enumerate(pairs)]
    for copy in copies:
        copy.start()
    slot_terms(h_ref, slot_ref, recv_ref, it_ref, loc_ref)
    for copy in copies:
        copy.wait()
    rim_one_hots(nb_ref, hot_ref)
    local_part(v_ref, j_ref, visc_ref, nb_ref, g_ref, h_ref, vt_ref, o_ref)


def second_local(
    v_ref, j_ref, visc_ref, nb_ref, g_ref, h_ref, slot_ref, recv_ref, vt_ref, it_ref,
    o_ref, loc_ref, v_hbm, sem,
):
    copy = pltpu.make_async_copy(v_ref, v_hbm, sem)
    copy.start()
    slot_terms(h_ref, slot_ref, recv_ref, it_ref, loc_ref)
    local_part(v_ref, j_ref, visc_ref, nb_ref, g_ref, h_ref, vt_ref, o_ref)
    copy.wait()


def middle_kernel(
    base_ref, edge_ref, hot_ref, slot_ref, recv_ref, j_ref, it_ref,
    o_ref, g_ref, h_ref, edge2_ref, m_hbm,
    m_ref, m_sems,
):
    edge_part(base_ref, edge_ref, hot_ref, o_ref)
    trace_part(o_ref, j_ref, g_ref, h_ref)
    send_part(g_ref, slot_ref[...], recv_ref, it_ref, edge2_ref, m_ref, m_hbm, m_sems)


def shape(*dims, kind=F32):
    return jax.ShapeDtypeStruct(dims, kind)


PARAMS = pltpu.CompilerParams(vmem_limit_bytes=32 * 1024 * 1024)


def call(kernel, outs, *args):
    return pl.pallas_call(kernel, out_shape=outs, compiler_params=PARAMS)(*args)


IMAGE = shape(5, 64, 128)
TRACES = shape(6, 80, 128)
EDGE = shape(120, 128)
SLOTS = shape(160, 128)
MESSAGE = shape(4, 160, 128)
SLOT_HOTS = shape(768, 256, kind=BF16)
RIM_HOTS = shape(6, 128, 128, kind=BF16)


def exchange(edge, message):
    ends = [(4 * c + 3, 4 * c + 4) for c in range(lax.axis_size("curve") - 1)]
    message = lax.all_to_all(message, "group", split_axis=0, concat_axis=0, tiled=True)
    edge = lax.ppermute(edge, AXES, ends + [(j, i) for i, j in ends])
    return edge, message


VMEM = pl.BlockSpec(memory_space=pltpu.VMEM)
HBM = pl.BlockSpec(memory_space=pltpu.HBM)
MESSAGE_SCRATCH = [pltpu.VMEM(MESSAGE.shape, F32)]
TWO_COPIES = pltpu.SemaphoreType.DMA((2,))


def in_hbm(*args):
    return [pltpu.with_memory_space_constraint(x, pltpu.HBM) for x in args]


def local(tangent, jacobian, viscosity, neighbours, send_table, recv_table):
    volume_table, inter_table, project_table = (jnp.asarray(t) for t in operator_tables())
    jacobian = jnp.transpose(jacobian, (1, 2, 0, 3))
    inputs = (tangent, jacobian, send_table, recv_table, inter_table)
    g, h, edge, message, slots, tangent, jacobian, recv_table, inter_table = pl.pallas_call(
        first_kernel,
        out_shape=(TRACES, TRACES, EDGE, MESSAGE, SLOT_HOTS)
        + tuple(pltpu.VMEM(inputs[i].shape, inputs[i].dtype) for i in (0, 1, 3, 4)),
        in_specs=[HBM] * 5,
        out_specs=(VMEM, VMEM, VMEM, HBM) + (VMEM,) * 5,
        scratch_shapes=[pltpu.VMEM(send_table.shape, send_table.dtype)]
        + MESSAGE_SCRATCH
        + [pltpu.SemaphoreType.DMA((5,)), TWO_COPIES],
        compiler_params=PARAMS,
    )(*in_hbm(*inputs))
    edge, message = exchange(edge, message)
    inputs = (viscosity, neighbours, volume_table, project_table)
    base, loc, hots, viscosity, neighbours, volume_table, project_table = pl.pallas_call(
        first_local,
        out_shape=(IMAGE, SLOTS, RIM_HOTS) + tuple(pltpu.VMEM(x.shape, x.dtype) for x in inputs),
        in_specs=[VMEM] * 7 + [HBM] * 4,
        out_specs=(VMEM,) * 7,
        scratch_shapes=[pltpu.SemaphoreType.DMA((4,))],
        compiler_params=PARAMS,
    )(tangent, jacobian, g, h, slots, recv_table, inter_table, *in_hbm(*inputs))
    base = call(group_part, IMAGE, base, loc, message, hots, slots, recv_table, project_table)
    image, g, h, edge, message = pl.pallas_call(
        middle_kernel,
        out_shape=(pltpu.VMEM(IMAGE.shape, F32), TRACES, TRACES, EDGE, MESSAGE),
        in_specs=[VMEM] * 7,
        out_specs=(VMEM, VMEM, VMEM, VMEM, HBM),
        scratch_shapes=MESSAGE_SCRATCH + [TWO_COPIES],
        compiler_params=PARAMS,
    )(base, edge, hots, slots, recv_table, jacobian, inter_table)
    edge, message = exchange(edge, message)
    base, loc, first = pl.pallas_call(
        second_local,
        out_shape=(IMAGE, SLOTS, IMAGE),
        in_specs=[VMEM] * 10,
        out_specs=(VMEM, VMEM, HBM),
        scratch_shapes=[pltpu.SemaphoreType.DMA],
        compiler_params=PARAMS,
    )(image, jacobian, viscosity, neighbours, g, h, slots, recv_table, volume_table, inter_table)
    base = call(group_part, IMAGE, base, loc, message, hots, slots, recv_table, project_table)
    second = call(edge_part, IMAGE, base, edge, hots)
    return first, second


def solution(mesh):
    in_specs = (
        P(None, None, AXES),
        P(None, None, None, AXES),
        P(AXES),
        P(None, AXES),
        P(None, AXES),
        P(None, AXES),
    )
    out_specs = (P(None, None, AXES), P(None, None, AXES))
    return jax.shard_map(local, mesh=mesh, in_specs=in_specs, out_specs=out_specs, check_vma=False)
```

```python
import jax
import jax.numpy as jnp
import ml_dtypes
import numpy as np
from jax import lax
from jax.experimental import pallas as pl
from jax.experimental.pallas import tpu as pltpu
from jax.sharding import PartitionSpec as P

F32 = jnp.float32
BF16 = jnp.bfloat16
AXES = ("curve", "group")
PSEUDO_STEP = 0.05
FACE_SCALE = 0.15


def node_tables():
    points = np.array([-1.0, -1.0 / np.sqrt(5.0), 1.0 / np.sqrt(5.0), 1.0])
    weights = np.array([1.0, 5.0, 5.0, 1.0]) / 6.0
    barycentric = np.array(
        [1.0 / np.prod([points[j] - points[k] for k in range(4) if k != j]) for j in range(4)]
    )
    derivative = np.zeros((4, 4))
    for a in range(4):
        for b in range(4):
            if a != b:
                derivative[a, b] = barycentric[b] / barycentric[a] / (points[a] - points[b])
        derivative[a, a] = -np.sum(derivative[a])
    halves = []
    for upper_half in range(2):
        matrix = np.zeros((4, 4))
        for a in range(4):
            target = 0.5 * points[a] + upper_half - 0.5
            for b in range(4):
                matrix[a, b] = np.prod(
                    [(target - points[k]) / (points[b] - points[k]) for k in range(4) if k != b]
                )
        halves.append(matrix)
    surface_weights = np.kron(weights, weights)
    interpolate = np.stack([np.kron(halves[c // 2], halves[c % 2]) for c in range(4)])
    project = np.stack(
        [
            0.25 * (interpolate[c].T * surface_weights[None, :]) / surface_weights[:, None]
            for c in range(4)
        ]
    )
    return derivative, interpolate, project


def pieces_of(matrix):
    hi = matrix.astype(ml_dtypes.bfloat16)
    lo = (matrix - hi.astype(np.float64)).astype(ml_dtypes.bfloat16)
    return np.concatenate([hi, hi, lo], axis=1)


def operator_tables():
    derivative, interpolate, project = node_tables()
    eye = np.eye(4)
    d_x = np.kron(eye, np.kron(eye, derivative))
    d_y = np.kron(eye, np.kron(derivative, eye))
    d_z = np.kron(derivative, np.kron(eye, eye))
    laplacian = d_x @ d_x + d_y @ d_y + d_z @ d_z
    volume = pieces_of(np.concatenate([d_x, d_y, d_z, laplacian], axis=0))
    return (
        volume,
        pieces_of(interpolate.reshape(64, 16)),
        pieces_of(project.reshape(64, 16)),
    )


def split(x):
    hi = x.astype(BF16)
    lo = (x - hi.astype(F32)).astype(BF16)
    return hi, lo


def dot(a, b):
    return lax.dot_general(a, b, (((1,), (0,)), ((), ())), preferred_element_type=F32)


def one_hot(index, rows):
    place = lax.broadcasted_iota(jnp.int32, (rows, index.shape[1]), 0)
    return jnp.where(place == index, 1.0, 0.0).astype(BF16)


def slot_one_hots(send_ref, recv_ref):
    fine = jnp.where(send_ref[2:3, :] > 0, send_ref[1:2, :] * 128 + send_ref[0:1, :], -1)
    coarse = jnp.where(recv_ref[3:4, :] > 0, recv_ref[1:2, :] * 128 + recv_ref[0:1, :], -1)
    return jnp.concatenate([one_hot(fine, 768), one_hot(coarse, 768)], axis=1)


def by_child(table_ref, values, recv_ref):
    count = len(values)
    hi, lo = split(jnp.concatenate(values, axis=1))
    product = dot(table_ref[...], jnp.concatenate([hi, lo, hi], axis=0))
    child = recv_ref[2:3, :]
    picks = [jnp.where(child == c, 1.0, 0.0) for c in range(4)]
    return [
        sum(
            product[16 * c : 16 * c + 16, 128 * n : 128 * n + 128] * picks[c]
            for c in range(4)
        )
        for n in range(count)
    ]


def face_values(v_ref, face, a):
    d, s = face // 2, face % 2
    if d == 0:
        return v_ref[a, pl.ds(3 * s, 16, stride=4), :]
    if d == 1:
        return jnp.concatenate(
            [v_ref[a, 16 * k + 12 * s : 16 * k + 12 * s + 4, :] for k in range(4)], axis=0
        )
    return v_ref[a, 48 * s : 48 * s + 16, :]


def add_to_face(o_ref, face, a, values):
    d, s = face // 2, face % 2
    if d == 0:
        o_ref[a, pl.ds(3 * s, 16, stride=4), :] += values
    elif d == 1:
        for k in range(4):
            row = 16 * k + 12 * s
            o_ref[a, row : row + 4, :] += values[4 * k : 4 * k + 4]
    else:
        o_ref[a, 48 * s : 48 * s + 16, :] += values


def rims(g):
    odd = jnp.concatenate([g[1], g[3], g[5]], axis=0)
    even = jnp.concatenate([g[0], g[2], g[4]], axis=0)
    lane = lax.broadcasted_iota(jnp.int32, (120, 128), 1)
    up = jnp.where(lane < 64, pltpu.roll(odd[:120], 64, 1), odd[120:])
    down = jnp.where(lane < 64, even[:120], pltpu.roll(even[120:], 64, 1))
    return up, down


def trace_part(v_ref, j_ref, g_ref, h_ref):
    values = []
    for f in range(6):
        d = f // 2
        w = [face_values(v_ref, f, b) for b in range(5)]
        parts = []
        for a in range(5):
            q = j_ref[a, 0, d : d + 1, :] * w[0]
            for b in range(1, 5):
                q = q + j_ref[a, b, d : d + 1, :] * w[b]
            rows = slice(16 * a, 16 * a + 16)
            plus, minus = w[a] + q, w[a] - q
            g, h = (plus, minus) if f % 2 else (minus, plus)
            g_ref[f, rows, :] = g
            h_ref[f, rows, :] = h
            parts.append(g)
        values.append(jnp.concatenate(parts, axis=0))
    return values


def pick_slots(t, hots):
    hi, lo = split(jnp.concatenate([t[f] for f in range(6)], axis=1))
    picked = dot(jnp.concatenate([hi, lo], axis=0), hots)
    return picked[:80], picked[80:]


def inter_slots(values, it_ref, recv_ref):
    rows = [values[16 * a : 16 * a + 16] for a in range(5)]
    return jnp.concatenate(by_child(it_ref, rows, recv_ref), axis=0)


def send_part(g, hots, recv_ref, it_ref, edge_ref, slots_ref, rims_ref, m_hbm, sems):
    me = lax.axis_index("group")
    up, down = rims(g)
    edge_ref[...] = jnp.where(me == 0, down, up)
    rims_ref[0] = down
    rims_ref[1] = up
    copies = [
        pltpu.make_async_copy(rims_ref.at[i], m_hbm.at[t, pl.ds(40, 120), :], sems.at[i])
        for i, t in enumerate((jnp.maximum(me - 1, 0), jnp.minimum(me + 1, 3)))
    ]
    for copy in copies:
        copy.start()
    hi, lo = pick_slots(g, hots)
    picked = hi + lo
    outgoing = jnp.concatenate(
        [picked[:, :128], inter_slots(picked[:, 128:], it_ref, recv_ref)], axis=0
    )
    quarter = lax.broadcasted_iota(jnp.int32, (40, 128), 1) // 32
    for t in range(4):
        block = None
        for q in range(4):
            part = outgoing[40 * q : 40 * q + 40]
            shift = (32 * (q - t)) % 128
            part = pltpu.roll(part, shift, 1) if shift else part
            block = part if block is None else jnp.where(quarter == q, part, block)
        slots_ref[t] = block
    copies.append(
        pltpu.make_async_copy(slots_ref, m_hbm.at[:, pl.ds(0, 40), :], sems.at[2])
    )
    copies[-1].start()
    return copies


def places(nb_ref, f):
    first_id = (lax.axis_index("curve") * 4 + lax.axis_index("group")) * 128
    linked = nb_ref[f : f + 1, :]
    return linked >= 0, linked - first_id


def rim_one_hots(nb_ref, hot_ref):
    for f in range(6):
        linked, place = places(nb_ref, f)
        place = place - 128 if f % 2 else place + 64
        rim = linked & (place >= 0 if f % 2 else place < 64)
        hot = one_hot(jnp.where(rim, place, -1), 64)
        hot_ref[f] = jnp.concatenate([hot, hot], axis=0)


def rim_pieces(packed):
    lane = lax.broadcasted_iota(jnp.int32, (120, 128), 1)
    hi = packed.astype(BF16).astype(F32)
    lo = packed - hi
    return jnp.concatenate(
        [
            jnp.where(lane < 64, hi, pltpu.roll(lo, 64, 1)),
            jnp.where(lane < 64, pltpu.roll(hi, 64, 1), lo),
        ],
        axis=0,
    ).astype(BF16)


def group_part(base_ref, loc_ref, m_ref, hot_ref, slot_ref, recv_ref, pt_ref, o_ref):
    me = lax.axis_index("group")
    quarter = lax.broadcasted_iota(jnp.int32, (40, 128), 1) // 32
    parts = []
    for q in range(4):
        part = None
        for s in range(4):
            shift = (32 * (s - q)) % 128
            block = m_ref[s, 0:40, :]
            block = pltpu.roll(block, shift, 1) if shift else block
            part = block if part is None else jnp.where(quarter == s, block, part)
        parts.append(part)
    incoming = jnp.concatenate(parts, axis=0) - loc_ref[...]
    projected = by_child(pt_ref, [incoming[16 * a : 16 * a + 16] for a in range(5)], recv_ref)
    values = jnp.concatenate([incoming[80:160], jnp.concatenate(projected, axis=0)], axis=1)
    hi, lo = split(values)
    spread = lax.dot_general(
        jnp.concatenate([hi, lo], axis=0),
        slot_ref[...],
        (((1,), (1,)), ((), ())),
        preferred_element_type=F32,
    )
    before = jnp.where(me == 0, 0.0, m_ref[jnp.maximum(me - 1, 0), 40:160, :])
    after = jnp.where(me == 3, 0.0, m_ref[jnp.minimum(me + 1, 3), 40:160, :])
    halos = [rim_pieces(before), rim_pieces(after)]
    o_ref[...] = base_ref[...]
    for f in range(6):
        third = f // 2
        far = dot(halos[f % 2][80 * third : 80 * third + 80], hot_ref[f])
        columns = slice(128 * f, 128 * f + 128)
        total = (far + spread[:80, columns] + spread[80:, columns]) * (-FACE_SCALE)
        for a in range(5):
            add_to_face(o_ref, f, a, total[16 * a : 16 * a + 16])


def edge_part(edge_ref, hot_ref, o_ref):
    me = lax.axis_index("group")
    for end, parity in ((0, 0), (3, 1)):

        @pl.when(me == end)
        def _():
            halo = rim_pieces(edge_ref[120 * parity : 120 * parity + 120, :])
            for third in range(3):
                f = 2 * third + parity
                far = dot(halo[80 * third : 80 * third + 80], hot_ref[f]) * (-FACE_SCALE)
                for a in range(5):
                    add_to_face(o_ref, f, a, far[16 * a : 16 * a + 16])


def slot_terms(h_ref, slot_ref, recv_ref, it_ref, loc_ref):
    hi, lo = pick_slots(h_ref, slot_ref[...])
    picked = hi + lo
    loc_ref[...] = jnp.concatenate(
        [inter_slots(picked[:, 128:], it_ref, recv_ref), picked[:, :128]], axis=0
    )


def local_part(v_ref, j_ref, visc_ref, nb_ref, g_ref, h_ref, vt_ref, o_ref):
    v = v_ref[...]
    hi, lo = split(jnp.concatenate([v[a] for a in range(5)], axis=1))
    terms = dot(vt_ref[...], jnp.concatenate([hi, lo, hi], axis=0))
    visc = visc_ref[...].reshape(1, 128)
    for a in range(5):
        total = visc * terms[192:256, 128 * a : 128 * a + 128]
        for d in range(3):
            for b in range(5):
                total = total - j_ref[a, b, d : d + 1, :] * terms[
                    64 * d : 64 * d + 64, 128 * b : 128 * b + 128
                ]
        o_ref[a] = v[a] - PSEUDO_STEP * total
    for f in range(6):
        linked, place = places(nb_ref, f)
        own = linked & (place < 128 if f % 2 else place >= 0)
        hi, lo = split(g_ref[f ^ 1])
        near = dot(jnp.concatenate([hi, lo], axis=0), one_hot(jnp.where(own, place, -1), 128))
        mask = jnp.where(nb_ref[f : f + 1, :] != -2, FACE_SCALE, 0.0)
        total = mask * h_ref[f] - FACE_SCALE * (near[:80] + near[80:])
        for a in range(5):
            add_to_face(o_ref, f, a, total[16 * a : 16 * a + 16])


def first_kernel(
    v_hbm, j_hbm, send_hbm, recv_hbm, it_hbm, visc_hbm, nb_hbm, vt_hbm, pt_hbm,
    edge_ref, m_hbm, slot_ref, base_ref, loc_ref, hot_ref,
    j_ref, recv_ref, it_ref, visc_ref, nb_ref, vt_ref, pt_ref,
    v_ref, send_ref, g_ref, h_ref, slots_ref, rims_ref, m_sems, sems,
):
    pairs = (
        (v_hbm, v_ref), (j_hbm, j_ref), (send_hbm, send_ref), (recv_hbm, recv_ref), (it_hbm, it_ref),
        (visc_hbm, visc_ref), (nb_hbm, nb_ref), (vt_hbm, vt_ref), (pt_hbm, pt_ref),
    )
    copies = [pltpu.make_async_copy(a, b, sems.at[i]) for i, (a, b) in enumerate(pairs)]
    for copy in copies:
        copy.start()
    for copy in copies[2:5]:
        copy.wait()
    slot_ref[...] = slot_one_hots(send_ref, recv_ref)
    for copy in copies[:2]:
        copy.wait()
    g = trace_part(v_ref, j_ref, g_ref, h_ref)
    sent = send_part(g, slot_ref[...], recv_ref, it_ref, edge_ref, slots_ref, rims_ref, m_hbm, m_sems)
    for copy in copies[5:]:
        copy.wait()
    rim_one_hots(nb_ref, hot_ref)
    slot_terms(h_ref, slot_ref, recv_ref, it_ref, loc_ref)
    local_part(v_ref, j_ref, visc_ref, nb_ref, g_ref, h_ref, vt_ref, base_ref)
    for copy in sent:
        copy.wait()


def middle_kernel(
    base_ref, loc_ref, m_ref, edge_ref, hot_ref, slot_ref,
    j_ref, recv_ref, it_ref, visc_ref, nb_ref, vt_ref, pt_ref,
    v_hbm, edge2_ref, m_hbm, base2_ref, loc2_ref,
    v_ref, g_ref, h_ref, slots_ref, rims_ref, m_sems, sem,
):
    group_part(base_ref, loc_ref, m_ref, hot_ref, slot_ref, recv_ref, pt_ref, v_ref)
    edge_part(edge_ref, hot_ref, v_ref)
    g = trace_part(v_ref, j_ref, g_ref, h_ref)
    sent = send_part(g, slot_ref[...], recv_ref, it_ref, edge2_ref, slots_ref, rims_ref, m_hbm, m_sems)
    image = pltpu.make_async_copy(v_ref, v_hbm, sem)
    image.start()
    slot_terms(h_ref, slot_ref, recv_ref, it_ref, loc2_ref)
    local_part(v_ref, j_ref, visc_ref, nb_ref, g_ref, h_ref, vt_ref, base2_ref)
    for copy in sent:
        copy.wait()
    image.wait()


def last_kernel(base_ref, loc_ref, m_ref, edge_ref, hot_ref, slot_ref, recv_ref, pt_ref, o_ref):
    group_part(base_ref, loc_ref, m_ref, hot_ref, slot_ref, recv_ref, pt_ref, o_ref)
    edge_part(edge_ref, hot_ref, o_ref)


def shape(*dims, kind=F32):
    return jax.ShapeDtypeStruct(dims, kind)


PARAMS = pltpu.CompilerParams(vmem_limit_bytes=32 * 1024 * 1024)


IMAGE = shape(5, 64, 128)
EDGE = shape(120, 128)
SLOTS = shape(160, 128)
MESSAGE = shape(4, 160, 128)
SLOT_HOTS = shape(768, 256, kind=BF16)
RIM_HOTS = shape(6, 128, 128, kind=BF16)


VMEM = pl.BlockSpec(memory_space=pltpu.VMEM)
HBM = pl.BlockSpec(memory_space=pltpu.HBM)
TRACES = pltpu.VMEM((6, 80, 128), F32)
SEND_SCRATCH = [
    TRACES,
    TRACES,
    pltpu.VMEM((4, 40, 128), F32),
    pltpu.VMEM((2, 120, 128), F32),
    pltpu.SemaphoreType.DMA((3,)),
]


def exchange(edge, message):
    count = lax.axis_size(AXES)
    pairs = [[0, 1], [count - 2, count - 1]]
    pairs += [[d + i, d + j] for d in range(0, count - 4, 4) for i, j in ((3, 4), (2, 5))]
    message = lax.all_to_all(message, "group", split_axis=0, concat_axis=0, tiled=True)
    edge = lax.all_gather(edge, AXES, axis_index_groups=pairs, axis=0, tiled=True)
    return edge, message


def local(tangent, jacobian, viscosity, neighbours, send_table, recv_table):
    volume_table, inter_table, project_table = (jnp.asarray(t) for t in operator_tables())
    inputs = (
        tangent, jnp.transpose(jacobian, (1, 2, 0, 3)), send_table, recv_table, inter_table,
        viscosity, neighbours, volume_table, project_table,
    )
    kept = [inputs[i] for i in (1, 3, 4, 5, 6, 7, 8)]
    edge, message, slots, base, loc, hots, *kept = pl.pallas_call(
        first_kernel,
        out_shape=(EDGE, MESSAGE, SLOT_HOTS, IMAGE, SLOTS, RIM_HOTS)
        + tuple(pltpu.VMEM(x.shape, x.dtype) for x in kept),
        in_specs=[HBM] * 9,
        out_specs=(VMEM, HBM) + (VMEM,) * 11,
        scratch_shapes=[
            pltpu.VMEM(tangent.shape, F32), pltpu.VMEM(send_table.shape, send_table.dtype)
        ]
        + SEND_SCRATCH
        + [pltpu.SemaphoreType.DMA((9,))],
        compiler_params=PARAMS,
    )(*(pltpu.with_memory_space_constraint(x, pltpu.HBM) for x in inputs))
    edge, message = exchange(edge, message)
    first, edge, message, base, loc = pl.pallas_call(
        middle_kernel,
        out_shape=(IMAGE, EDGE, MESSAGE, IMAGE, SLOTS),
        in_specs=[VMEM] * 13,
        out_specs=(HBM, VMEM, HBM, VMEM, VMEM),
        scratch_shapes=[pltpu.VMEM(IMAGE.shape, F32)] + SEND_SCRATCH + [pltpu.SemaphoreType.DMA],
        compiler_params=PARAMS,
    )(base, loc, message, edge, hots, slots, *kept)
    edge, message = exchange(edge, message)
    recv_table, project_table = kept[1], kept[6]
    second = pl.pallas_call(
        last_kernel, out_shape=IMAGE, in_specs=[VMEM] * 8, out_specs=VMEM, compiler_params=PARAMS
    )(base, loc, message, edge, hots, slots, recv_table, project_table)
    return first, second


def solution(mesh):
    in_specs = (
        P(None, None, AXES),
        P(None, None, None, AXES),
        P(AXES),
        P(None, AXES),
        P(None, AXES),
        P(None, AXES),
    )
    out_specs = (P(None, None, AXES), P(None, None, AXES))
    return jax.shard_map(local, mesh=mesh, in_specs=in_specs, out_specs=out_specs, check_vma=False)
```

```python
import jax
import jax.numpy as jnp
import ml_dtypes
import numpy as np
from jax import lax
from jax.experimental import pallas as pl
from jax.experimental.pallas import tpu as pltpu
from jax.sharding import PartitionSpec as P

F32 = jnp.float32
BF16 = jnp.bfloat16
AXES = ("curve", "group")
PSEUDO_STEP = 0.05
FACE_SCALE = 0.15


def node_tables():
    points = np.array([-1.0, -1.0 / np.sqrt(5.0), 1.0 / np.sqrt(5.0), 1.0])
    weights = np.array([1.0, 5.0, 5.0, 1.0]) / 6.0
    barycentric = np.array(
        [1.0 / np.prod([points[j] - points[k] for k in range(4) if k != j]) for j in range(4)]
    )
    derivative = np.zeros((4, 4))
    for a in range(4):
        for b in range(4):
            if a != b:
                derivative[a, b] = barycentric[b] / barycentric[a] / (points[a] - points[b])
        derivative[a, a] = -np.sum(derivative[a])
    halves = []
    for upper_half in range(2):
        matrix = np.zeros((4, 4))
        for a in range(4):
            target = 0.5 * points[a] + upper_half - 0.5
            for b in range(4):
                matrix[a, b] = np.prod(
                    [(target - points[k]) / (points[b] - points[k]) for k in range(4) if k != b]
                )
        halves.append(matrix)
    surface_weights = np.kron(weights, weights)
    interpolate = np.stack([np.kron(halves[c // 2], halves[c % 2]) for c in range(4)])
    project = np.stack(
        [
            0.25 * (interpolate[c].T * surface_weights[None, :]) / surface_weights[:, None]
            for c in range(4)
        ]
    )
    return derivative, interpolate, project


def pieces_of(matrix):
    hi = matrix.astype(ml_dtypes.bfloat16)
    lo = (matrix - hi.astype(np.float64)).astype(ml_dtypes.bfloat16)
    return np.concatenate([hi, hi, lo], axis=1)


def operator_tables():
    derivative, interpolate, project = node_tables()
    eye = np.eye(4)
    d_x = np.kron(eye, np.kron(eye, derivative))
    d_y = np.kron(eye, np.kron(derivative, eye))
    d_z = np.kron(derivative, np.kron(eye, eye))
    laplacian = d_x @ d_x + d_y @ d_y + d_z @ d_z
    volume = pieces_of(np.concatenate([d_x, d_y, d_z, laplacian], axis=0))
    return (
        volume,
        pieces_of(interpolate.reshape(64, 16)),
        pieces_of(project.reshape(64, 16)),
    )


def split(x):
    hi = x.astype(BF16)
    lo = (x - hi.astype(F32)).astype(BF16)
    return hi, lo


def dot(a, b):
    return lax.dot_general(a, b, (((1,), (0,)), ((), ())), preferred_element_type=F32)


def one_hot(index, rows):
    place = lax.broadcasted_iota(jnp.int32, (rows, index.shape[1]), 0)
    return jnp.where(place == index, 1.0, 0.0).astype(BF16)


def slot_one_hots(send_ref, recv_ref):
    fine = jnp.where(send_ref[2:3, :] > 0, send_ref[1:2, :] * 128 + send_ref[0:1, :], -1)
    coarse = jnp.where(recv_ref[3:4, :] > 0, recv_ref[1:2, :] * 128 + recv_ref[0:1, :], -1)
    return jnp.concatenate([one_hot(fine, 768), one_hot(coarse, 768)], axis=1)


def by_child(table_ref, values, recv_ref):
    count = len(values)
    hi, lo = split(jnp.concatenate(values, axis=1))
    product = dot(table_ref[...], jnp.concatenate([hi, lo, hi], axis=0))
    child = recv_ref[2:3, :]
    picks = [jnp.where(child == c, 1.0, 0.0) for c in range(4)]
    return [
        sum(
            product[16 * c : 16 * c + 16, 128 * n : 128 * n + 128] * picks[c]
            for c in range(4)
        )
        for n in range(count)
    ]


def face_values(v_ref, face, a):
    d, s = face // 2, face % 2
    if d == 0:
        return v_ref[a, pl.ds(3 * s, 16, stride=4), :]
    if d == 1:
        return jnp.concatenate(
            [v_ref[a, 16 * k + 12 * s : 16 * k + 12 * s + 4, :] for k in range(4)], axis=0
        )
    return v_ref[a, 48 * s : 48 * s + 16, :]


def add_to_face(o_ref, face, a, values):
    d, s = face // 2, face % 2
    if d == 0:
        o_ref[a, pl.ds(3 * s, 16, stride=4), :] += values
    elif d == 1:
        for k in range(4):
            row = 16 * k + 12 * s
            o_ref[a, row : row + 4, :] += values[4 * k : 4 * k + 4]
    else:
        o_ref[a, 48 * s : 48 * s + 16, :] += values


def rims(g):
    odd = jnp.concatenate([g[1], g[3], g[5]], axis=0)
    even = jnp.concatenate([g[0], g[2], g[4]], axis=0)
    lane = lax.broadcasted_iota(jnp.int32, (120, 128), 1)
    up = jnp.where(lane < 64, pltpu.roll(odd[:120], 64, 1), odd[120:])
    down = jnp.where(lane < 64, even[:120], pltpu.roll(even[120:], 64, 1))
    return up, down


def trace_part(v_ref, j_ref, g_ref, h_ref):
    values = []
    for f in range(6):
        d = f // 2
        w = [face_values(v_ref, f, b) for b in range(5)]
        parts = []
        for a in range(5):
            q = j_ref[a, 0, d : d + 1, :] * w[0]
            for b in range(1, 5):
                q = q + j_ref[a, b, d : d + 1, :] * w[b]
            rows = slice(16 * a, 16 * a + 16)
            plus, minus = w[a] + q, w[a] - q
            g, h = (plus, minus) if f % 2 else (minus, plus)
            g_ref[f, rows, :] = g
            h_ref[f, rows, :] = h
            parts.append(g)
        values.append(jnp.concatenate(parts, axis=0))
    return values


def pick_slots(t, hots):
    hi, lo = split(jnp.concatenate([t[f] for f in range(6)], axis=1))
    picked = dot(jnp.concatenate([hi, lo], axis=0), hots)
    return picked[:80], picked[80:]


def inter_slots(values, it_ref, recv_ref):
    rows = [values[16 * a : 16 * a + 16] for a in range(5)]
    return jnp.concatenate(by_child(it_ref, rows, recv_ref), axis=0)


def send_part(g, hots, recv_ref, it_ref, edge_ref, slots_ref, rims_ref, m_hbm, sems):
    me = lax.axis_index("group")
    up, down = rims(g)
    edge_ref[...] = jnp.where(me == 0, down, up)
    rims_ref[0] = down
    rims_ref[1] = up
    copies = [
        pltpu.make_async_copy(rims_ref.at[i], m_hbm.at[t, pl.ds(40, 120), :], sems.at[i])
        for i, t in enumerate((jnp.maximum(me - 1, 0), jnp.minimum(me + 1, 3)))
    ]
    for copy in copies:
        copy.start()
    hi, lo = pick_slots(g, hots)
    picked = hi + lo
    outgoing = jnp.concatenate(
        [picked[:, :128], inter_slots(picked[:, 128:], it_ref, recv_ref)], axis=0
    )
    quarter = lax.broadcasted_iota(jnp.int32, (40, 128), 1) // 32
    for t in range(4):
        block = None
        for q in range(4):
            part = outgoing[40 * q : 40 * q + 40]
            shift = (32 * (q - t)) % 128
            part = pltpu.roll(part, shift, 1) if shift else part
            block = part if block is None else jnp.where(quarter == q, part, block)
        slots_ref[t] = block
    copies.append(
        pltpu.make_async_copy(slots_ref, m_hbm.at[:, pl.ds(0, 40), :], sems.at[2])
    )
    copies[-1].start()
    return copies


def places(nb_ref, f):
    first_id = (lax.axis_index("curve") * 4 + lax.axis_index("group")) * 128
    linked = nb_ref[f : f + 1, :]
    return linked >= 0, linked - first_id


def rim_one_hots(nb_ref, hot_ref):
    for f in range(6):
        linked, place = places(nb_ref, f)
        place = place - 128 if f % 2 else place + 64
        rim = linked & (place >= 0 if f % 2 else place < 64)
        hot = one_hot(jnp.where(rim, place, -1), 64)
        hot_ref[f] = jnp.concatenate([hot, hot], axis=0)


def rim_pieces(packed):
    lane = lax.broadcasted_iota(jnp.int32, (120, 128), 1)
    hi = packed.astype(BF16).astype(F32)
    lo = packed - hi
    return jnp.concatenate(
        [
            jnp.where(lane < 64, hi, pltpu.roll(lo, 64, 1)),
            jnp.where(lane < 64, pltpu.roll(hi, 64, 1), lo),
        ],
        axis=0,
    ).astype(BF16)


def group_part(base_ref, loc_ref, m_ref, hot_ref, slot_ref, recv_ref, pt_ref, o_ref):
    me = lax.axis_index("group")
    quarter = lax.broadcasted_iota(jnp.int32, (40, 128), 1) // 32
    parts = []
    for q in range(4):
        part = None
        for s in range(4):
            shift = (32 * (s - q)) % 128
            block = m_ref[s, 0:40, :]
            block = pltpu.roll(block, shift, 1) if shift else block
            part = block if part is None else jnp.where(quarter == s, block, part)
        parts.append(part)
    incoming = jnp.concatenate(parts, axis=0) - loc_ref[...]
    projected = by_child(pt_ref, [incoming[16 * a : 16 * a + 16] for a in range(5)], recv_ref)
    values = jnp.concatenate([incoming[80:160], jnp.concatenate(projected, axis=0)], axis=1)
    hi, lo = split(values)
    spread = lax.dot_general(
        jnp.concatenate([hi, lo], axis=0),
        slot_ref[...],
        (((1,), (1,)), ((), ())),
        preferred_element_type=F32,
    )
    before = jnp.where(me == 0, 0.0, m_ref[jnp.maximum(me - 1, 0), 40:160, :])
    after = jnp.where(me == 3, 0.0, m_ref[jnp.minimum(me + 1, 3), 40:160, :])
    halos = [rim_pieces(before), rim_pieces(after)]
    o_ref[...] = base_ref[...]
    for f in range(6):
        third = f // 2
        far = dot(halos[f % 2][80 * third : 80 * third + 80], hot_ref[f])
        columns = slice(128 * f, 128 * f + 128)
        total = (far + spread[:80, columns] + spread[80:, columns]) * (-FACE_SCALE)
        for a in range(5):
            add_to_face(o_ref, f, a, total[16 * a : 16 * a + 16])


def edge_part(edge_ref, hot_ref, o_ref):
    me = lax.axis_index("group")
    for end, parity in ((0, 0), (3, 1)):

        @pl.when(me == end)
        def _():
            halo = rim_pieces(edge_ref[120 * parity : 120 * parity + 120, :])
            for third in range(3):
                f = 2 * third + parity
                far = dot(halo[80 * third : 80 * third + 80], hot_ref[f]) * (-FACE_SCALE)
                for a in range(5):
                    add_to_face(o_ref, f, a, far[16 * a : 16 * a + 16])


def slot_terms(h_ref, slot_ref, recv_ref, it_ref, loc_ref):
    hi, lo = pick_slots(h_ref, slot_ref[...])
    picked = hi + lo
    loc_ref[...] = jnp.concatenate(
        [inter_slots(picked[:, 128:], it_ref, recv_ref), picked[:, :128]], axis=0
    )


def local_part(v_ref, j_ref, visc_ref, nb_ref, g_ref, h_ref, vt_ref, o_ref):
    v = v_ref[...]
    hi, lo = split(jnp.concatenate([v[a] for a in range(5)], axis=1))
    terms = dot(vt_ref[...], jnp.concatenate([hi, lo, hi], axis=0))
    visc = visc_ref[...].reshape(1, 128)
    for a in range(5):
        total = visc * terms[192:256, 128 * a : 128 * a + 128]
        for d in range(3):
            for b in range(5):
                total = total - j_ref[a, b, d : d + 1, :] * terms[
                    64 * d : 64 * d + 64, 128 * b : 128 * b + 128
                ]
        o_ref[a] = v[a] - PSEUDO_STEP * total
    for f in range(6):
        linked, place = places(nb_ref, f)
        own = linked & (place < 128 if f % 2 else place >= 0)
        hi, lo = split(g_ref[f ^ 1])
        near = dot(jnp.concatenate([hi, lo], axis=0), one_hot(jnp.where(own, place, -1), 128))
        mask = jnp.where(nb_ref[f : f + 1, :] != -2, FACE_SCALE, 0.0)
        total = mask * h_ref[f] - FACE_SCALE * (near[:80] + near[80:])
        for a in range(5):
            add_to_face(o_ref, f, a, total[16 * a : 16 * a + 16])


def first_kernel(
    v_hbm, j_hbm, send_hbm, recv_hbm, it_hbm, visc_hbm, nb_hbm, vt_hbm, pt_hbm,
    edge_ref, m_hbm, slot_ref, base_ref, loc_ref, hot_ref,
    j_ref, recv_ref, it_ref, visc_ref, nb_ref, vt_ref, pt_ref,
    v_ref, send_ref, g_ref, h_ref, slots_ref, rims_ref, m_sems, sems,
):
    pairs = (
        (v_hbm, v_ref), (j_hbm, j_ref), (send_hbm, send_ref), (recv_hbm, recv_ref), (it_hbm, it_ref),
        (visc_hbm, visc_ref), (nb_hbm, nb_ref), (vt_hbm, vt_ref), (pt_hbm, pt_ref),
    )
    copies = [pltpu.make_async_copy(a, b, sems.at[i]) for i, (a, b) in enumerate(pairs)]
    for copy in copies:
        copy.start()
    for copy in copies[2:5]:
        copy.wait()
    slot_ref[...] = slot_one_hots(send_ref, recv_ref)
    for copy in copies[:2]:
        copy.wait()
    g = trace_part(v_ref, j_ref, g_ref, h_ref)
    sent = send_part(g, slot_ref[...], recv_ref, it_ref, edge_ref, slots_ref, rims_ref, m_hbm, m_sems)
    for copy in copies[5:]:
        copy.wait()
    rim_one_hots(nb_ref, hot_ref)
    slot_terms(h_ref, slot_ref, recv_ref, it_ref, loc_ref)
    local_part(v_ref, j_ref, visc_ref, nb_ref, g_ref, h_ref, vt_ref, base_ref)
    for copy in sent:
        copy.wait()


def middle_kernel(
    base_ref, loc_ref, m_ref, edge_ref, hot_ref, slot_ref,
    j_ref, recv_ref, it_ref, visc_ref, nb_ref, vt_ref, pt_ref,
    v_ref, edge2_ref, m_hbm, base2_ref, loc2_ref,
    g_ref, h_ref, slots_ref, rims_ref, m_sems,
):
    group_part(base_ref, loc_ref, m_ref, hot_ref, slot_ref, recv_ref, pt_ref, v_ref)
    edge_part(edge_ref, hot_ref, v_ref)
    g = trace_part(v_ref, j_ref, g_ref, h_ref)
    sent = send_part(g, slot_ref[...], recv_ref, it_ref, edge2_ref, slots_ref, rims_ref, m_hbm, m_sems)
    slot_terms(h_ref, slot_ref, recv_ref, it_ref, loc2_ref)
    local_part(v_ref, j_ref, visc_ref, nb_ref, g_ref, h_ref, vt_ref, base2_ref)
    for copy in sent:
        copy.wait()


def last_kernel(
    v_ref, base_ref, loc_ref, m_ref, edge_ref, hot_ref, slot_ref, recv_ref, pt_ref,
    v_hbm, o_ref, sem,
):
    image = pltpu.make_async_copy(v_ref, v_hbm, sem)
    image.start()
    group_part(base_ref, loc_ref, m_ref, hot_ref, slot_ref, recv_ref, pt_ref, o_ref)
    edge_part(edge_ref, hot_ref, o_ref)
    image.wait()


def shape(*dims, kind=F32):
    return jax.ShapeDtypeStruct(dims, kind)


PARAMS = pltpu.CompilerParams(vmem_limit_bytes=32 * 1024 * 1024)


IMAGE = shape(5, 64, 128)
EDGE = shape(120, 128)
SLOTS = shape(160, 128)
MESSAGE = shape(4, 160, 128)
SLOT_HOTS = shape(768, 256, kind=BF16)
RIM_HOTS = shape(6, 128, 128, kind=BF16)


VMEM = pl.BlockSpec(memory_space=pltpu.VMEM)
HBM = pl.BlockSpec(memory_space=pltpu.HBM)
TRACES = pltpu.VMEM((6, 80, 128), F32)
SEND_SCRATCH = [
    TRACES,
    TRACES,
    pltpu.VMEM((4, 40, 128), F32),
    pltpu.VMEM((2, 120, 128), F32),
    pltpu.SemaphoreType.DMA((3,)),
]


def exchange(edge, message):
    count = lax.axis_size(AXES)
    pairs = [[0, 1], [count - 2, count - 1]]
    pairs += [[d + i, d + j] for d in range(0, count - 4, 4) for i, j in ((3, 4), (2, 5))]
    message = lax.all_to_all(message, "group", split_axis=0, concat_axis=0, tiled=True)
    edge = lax.all_gather(edge, AXES, axis_index_groups=pairs, axis=0, tiled=True)
    return edge, message


def local(tangent, jacobian, viscosity, neighbours, send_table, recv_table):
    volume_table, inter_table, project_table = (jnp.asarray(t) for t in operator_tables())
    inputs = (
        tangent, jnp.transpose(jacobian, (1, 2, 0, 3)), send_table, recv_table, inter_table,
        viscosity, neighbours, volume_table, project_table,
    )
    kept = [inputs[i] for i in (1, 3, 4, 5, 6, 7, 8)]
    edge, message, slots, base, loc, hots, *kept = pl.pallas_call(
        first_kernel,
        out_shape=(EDGE, MESSAGE, SLOT_HOTS, IMAGE, SLOTS, RIM_HOTS)
        + tuple(pltpu.VMEM(x.shape, x.dtype) for x in kept),
        in_specs=[HBM] * 9,
        out_specs=(VMEM, HBM) + (VMEM,) * 11,
        scratch_shapes=[
            pltpu.VMEM(tangent.shape, F32), pltpu.VMEM(send_table.shape, send_table.dtype)
        ]
        + SEND_SCRATCH
        + [pltpu.SemaphoreType.DMA((9,))],
        compiler_params=PARAMS,
    )(*(pltpu.with_memory_space_constraint(x, pltpu.HBM) for x in inputs))
    edge, message = exchange(edge, message)
    image, edge, message, base, loc = pl.pallas_call(
        middle_kernel,
        out_shape=(pltpu.VMEM(IMAGE.shape, F32), EDGE, MESSAGE, IMAGE, SLOTS),
        in_specs=[VMEM] * 13,
        out_specs=(VMEM, VMEM, HBM, VMEM, VMEM),
        scratch_shapes=SEND_SCRATCH,
        compiler_params=PARAMS,
    )(base, loc, message, edge, hots, slots, *kept)
    edge, message = exchange(edge, message)
    recv_table, project_table = kept[1], kept[6]
    first, second = pl.pallas_call(
        last_kernel,
        out_shape=(IMAGE, IMAGE),
        in_specs=[VMEM] * 9,
        out_specs=(HBM, VMEM),
        scratch_shapes=[pltpu.SemaphoreType.DMA],
        compiler_params=PARAMS,
    )(image, base, loc, message, edge, hots, slots, recv_table, project_table)
    return first, second


def solution(mesh):
    in_specs = (
        P(None, None, AXES),
        P(None, None, None, AXES),
        P(AXES),
        P(None, AXES),
        P(None, AXES),
        P(None, AXES),
    )
    out_specs = (P(None, None, AXES), P(None, None, AXES))
    return jax.shard_map(local, mesh=mesh, in_specs=in_specs, out_specs=out_specs, check_vma=False)
```
